128 devices in a mesh: row: 16 (over y, x), col: 8 (over z, core).
Axes of the slice: x: 4, y: 4, z: 4, core: 2. Of those that a mesh axis runs over, the one named last changes fastest.
Arguments:
- grid_obs: float32 [32, 4096, 1024], P(None, 'row', 'col'), may hold values from -6 to 6
- grid_noise: float32 [4096, 1024], P('row', 'col'), may hold values from 0.25 to 2
- station_obs: float32 [32, 16, 8, 1024], P(None, 'row', 'col'), may hold values from -6 to 6
- station_noise: float32 [16, 8, 1024], P('row', 'col'), may hold values from 0.25 to 2
- station_offset: float32 [2, 16, 8, 1024], P(None, 'row', 'col'), may hold values from 0 to 1
- station_cell: int32 [16, 8, 1024], P('row', 'col'), may hold values from 0 to 32638, as said below
- station_count: int32 [16, 8], P('row', 'col'), may hold values from 128 to 1024, as said below
- time_cov: float32 [32, 32], replicated, as said below
Outputs:
- solution_grid: float32 [32, 4096, 1024], P(None, 'row', 'col')
- solution_stations: float32 [32, 16, 8, 1024], P(None, 'row', 'col')
- residual_grid: float32 [32, 4096, 1024], P(None, 'row', 'col')
The draws below stay inside these ranges and needn't reach their ends.
Inputs may be any that keep to these rules, and one draw needn't show every extreme that they name: `station_cell`: cell r * 128 + c with r < 255 and c < 127, so the footprint lies in the station's tile. `station_count`: each tile holds 1024, 512, 256 or 128 stations. `time_cov`: symmetric; each diagonal entry exceeds the sum of the magnitudes of the other entries of its row.
All inputs are finite; a program needn't handle non-finite values.
Results may differ from the reference program's by a relative error of at most 0.00019.
Values sent between devices are 32-bit elements; how exact they have to be, the bound alone decides.
A program may use at most 128 MiB of HBM per device.

```python
import math
import jax
import jax.numpy as jnp
from jax import lax

CX = 256
CY = 128
STEPS = 32
SLOT = 1024
REACH = 8
ITERS = 2
NX = 4096
NY = 1024
N_ROW = 16
N_COL = 8


def draw_station_cell(key, part):
    first_key = jax.random.fold_in(key, 11)
    second_key = jax.random.fold_in(key, 12)
    rows_drawn = jax.random.randint(first_key, (N_ROW, N_COL, SLOT), 0, CX - 1, dtype=jnp.int32)
    cols_drawn = jax.random.randint(second_key, (N_ROW, N_COL, SLOT), 0, CY - 1, dtype=jnp.int32)
    cells = rows_drawn * CY + cols_drawn
    cells = cells.at[0, 0, 0].set(0)
    cells = cells.at[N_ROW - 1, N_COL - 1, SLOT - 1].set((CX - 2) * CY + CY - 2)
    return cells.astype(jnp.int32)


def draw_station_count(key, part):
    level_key = jax.random.fold_in(key, 21)
    pick_key = jax.random.fold_in(key, 22)
    levels = jax.random.randint(level_key, (N_ROW * N_COL,), 0, 4, dtype=jnp.int32)
    counts = SLOT // jnp.left_shift(jnp.ones_like(levels), levels)
    chosen = jax.random.randint(pick_key, (), 0, N_ROW * N_COL, dtype=jnp.int32)
    counts = counts.at[chosen].set(SLOT)
    counts = counts.at[(chosen + 1) % (N_ROW * N_COL)].set(SLOT // 8)
    return counts.reshape(N_ROW, N_COL).astype(jnp.int32)


def draw_time_cov(key, part):
    off_key = jax.random.fold_in(key, 31)
    diag_key = jax.random.fold_in(key, 32)
    spread = jax.random.uniform(off_key, (STEPS, STEPS), jnp.float32, -1.0, 1.0) / STEPS
    diagonal = jax.random.uniform(diag_key, (STEPS,), jnp.float32, 1.0, 1.5)
    symmetric = 0.5 * (spread + spread.T)
    symmetric = symmetric * (1.0 - jnp.eye(STEPS, dtype=jnp.float32))
    return (symmetric + jnp.diag(diagonal)).astype(jnp.float32)


def steps_of(key, shape, pieces, low, top_value):
    level, own = 1.0, jax.random.fold_in(key, 6)
    for dim, blocks in pieces:
        draws = jnp.exp(jax.random.uniform(jax.random.fold_in(own, dim), (blocks,), jnp.float32, low / len(pieces), top_value / len(pieces)))
        level = level * jnp.repeat(draws, shape[dim] // blocks).reshape([-1 if axis == dim else 1 for axis in range(len(shape))])
    return level


def scatter_about(own_key, dims, width, most, split=(), kind=jnp.bfloat16):
    array = width * jax.random.normal(own_key, dims, jnp.float32)
    if split:
        array = array * steps_of(own_key, dims, split, -0.22, 0.18)
    return jnp.clip(array, -most, most).astype(kind)


def setup_inputs(seed: int = 0) -> dict:
    splits = jax.random.split(jax.random.key(seed), 9)
    grid_obs = scatter_about(splits[0], (STEPS, NX, NY), 1.0, 6.0, ((1, 16), (2, 8)), jnp.float32)
    grid_noise = jnp.clip(jnp.exp(math.log(2.0) - 2.0794415 * jax.random.uniform(splits[1], (NX, NY), jnp.float32) ** steps_of(splits[1], (NX, NY), ((0, 16), (1, 8)), -0.2, 0.2)), 0.25, 2.0)
    station_obs = scatter_about(splits[2], (STEPS, N_ROW, N_COL, SLOT), 1.0, 6.0, ((1, 16), (2, 8)), jnp.float32)
    station_noise = jnp.clip(jnp.exp(math.log(2.0) - 2.0794415 * jax.random.uniform(splits[3], (N_ROW, N_COL, SLOT), jnp.float32) ** steps_of(splits[3], (N_ROW, N_COL, SLOT), ((0, 16), (1, 8)), -0.2, 0.2)), 0.25, 2.0)
    station_offset = jnp.clip(1.0 * jax.random.uniform(splits[4], (2, N_ROW, N_COL, SLOT), jnp.float32) ** steps_of(splits[4], (2, N_ROW, N_COL, SLOT), ((1, 16), (2, 8)), -0.2, 0.2), 0.0, 1.0)
    station_cell = draw_station_cell(jax.random.fold_in(splits[8], 71), 0)
    station_count = draw_station_count(jax.random.fold_in(splits[8], 71), 0)
    time_cov = draw_time_cov(jax.random.fold_in(splits[8], 71), 0)
    return dict(grid_obs=grid_obs, grid_noise=grid_noise, station_obs=station_obs, station_noise=station_noise, station_offset=station_offset, station_cell=station_cell, station_count=station_count, time_cov=time_cov)


def taper(reach):
    spread = jnp.abs(jnp.arange(-reach, reach + 1, dtype=jnp.int32)).astype(jnp.float32)
    return (1.0 - spread / (reach + 1)) * jnp.exp(-spread / 3.0)


def smooth_axis(field, weights, axis, length):
    padding = [(0, 0), (0, 0), (0, 0)]
    padding[axis] = (REACH, REACH)
    padded = jnp.pad(field, padding)
    total = jnp.zeros_like(field)
    for offset in range(2 * REACH + 1):
        total = total + weights[offset] * lax.slice_in_dim(padded, offset, offset + length, axis=1 if axis == 1 else 2)
    return total


def reference(grid_obs, grid_noise, station_obs, station_noise, station_offset, station_cell, station_count, time_cov):
    weights = taper(REACH)
    tile_row = (jnp.arange(N_ROW, dtype=jnp.int32) * CX)[:, None, None]
    tile_col = (jnp.arange(N_COL, dtype=jnp.int32) * CY)[None, :, None]
    cell_row = station_cell // CY
    cell_col = station_cell % CY
    base = ((tile_row + cell_row) * NY + tile_col + cell_col).astype(jnp.int32)
    station_indices = jnp.stack([base, base + NY, base + 1, base + NY + 1]).reshape(-1).astype(jnp.int32)
    along_row = station_offset[0]
    along_col = station_offset[1]
    footprint = jnp.stack([(1.0 - along_row) * (1.0 - along_col), along_row * (1.0 - along_col),
                           (1.0 - along_row) * along_col, along_row * along_col])
    live = (jnp.arange(SLOT, dtype=jnp.int32)[None, None, :] < station_count[:, :, None]).astype(jnp.float32)[None]

    def operate(grid_part, site_part):
        scattered = (footprint[None] * (live * site_part)[:, None]).reshape(STEPS, -1)
        merged = grid_part.reshape(STEPS, -1).at[:, station_indices].add(scattered).reshape(STEPS, NX, NY)
        temporal_shift = jnp.einsum("st,tij->sij", time_cov, merged, precision=lax.Precision.HIGHEST)
        smooth = smooth_axis(smooth_axis(temporal_shift, weights, 1, NX), weights, 2, NY)
        picked = smooth.reshape(STEPS, -1)[:, station_indices].reshape((STEPS, 4) + site_part.shape[1:])
        sampled = jnp.sum(footprint[None] * picked, axis=1)
        grid_out = 0.25 * smooth + grid_noise[None] * grid_part
        site_out = live * (0.25 * sampled + station_noise[None] * site_part) + (1.0 - live) * site_part
        return grid_out, site_out

    def inner(first, second):
        return jnp.sum(first[0] * second[0]) + jnp.sum(first[1] * second[1])

    def combine(scale, first, second):
        return (first[0] + scale * second[0], first[1] + scale * second[1])

    residual_vector = (grid_obs, live * station_obs)
    solution = (jnp.zeros_like(grid_obs), jnp.zeros_like(station_obs))
    direction = residual_vector
    norm_now = inner(residual_vector, residual_vector)
    for iteration in range(ITERS):
        image = operate(direction[0], direction[1])
        alpha = norm_now / inner(direction, image)
        solution = combine(alpha, solution, direction)
        residual_vector = combine(-alpha, residual_vector, image)
        norm_next = inner(residual_vector, residual_vector)
        direction = combine(norm_next / norm_now, residual_vector, direction)
        norm_now = norm_next
    return solution[0], solution[1], residual_vector[0]
```

```python
import functools

import jax
import jax.numpy as jnp
from jax import lax
from jax.experimental import pallas as pl
from jax.experimental.pallas import tpu as pltpu
from jax.sharding import PartitionSpec as P

REACH = 8
CX = 256
CY = 128
STEPS = 32
SLOT = 1024
CHUNK = 128
CHUNKS = SLOT // CHUNK
GROUPS = CX // 8
PAIRS = GROUPS + 2 * CHUNKS - 2
ZERO = PAIRS + 1
HIGH = CX + 2 * REACH
MESH = pl.DeviceIdType.MESH
f32, bf16, i32 = jnp.float32, jnp.bfloat16, jnp.int32


def iota(shape, dim):
    return lax.broadcasted_iota(i32, shape, dim)


def taper(offset):
    distance = jnp.abs(offset)
    spread = distance.astype(f32)
    value = (1.0 - spread / (REACH + 1)) * jnp.exp(-spread / 3.0)
    return jnp.where(distance <= REACH, value, 0.0)


def split(x):
    high = x.astype(bf16)
    return high, (x - high.astype(f32)).astype(bf16)


def both(x):
    return jnp.concatenate(split(x), axis=1)


def three(x):
    high = x.astype(bf16)
    rest = x - high.astype(f32)
    middle = rest.astype(bf16)
    return jnp.concatenate([high, middle, (rest - middle.astype(f32)).astype(bf16)], axis=0)


def dot(a, b):
    return lax.dot_general(a, b, (((1,), (0,)), ((), ())), preferred_element_type=f32)


def dot_nt(a, b):
    return lax.dot_general(a, b, (((1,), (1,)), ((), ())), preferred_element_type=f32)


def halves(x):
    return x[:, :CY] + x[:, CY:]


def fold(x):
    rows, cols = x.shape
    total = jnp.zeros((8, CY), f32)
    for c in range(cols // CY):
        total = total + jnp.sum(x[:, c * CY : (c + 1) * CY].reshape(rows // 8, 8, CY), axis=0)
    return total


def lane_step(lane, side):
    pair = lane >> 7
    place = (lane >> 3) & 15
    slot, odd = place >> 1, place & 1
    if side == 0:
        return 16 * pair + 8 * odd + slot
    return 16 * pair + jnp.where(odd == 1, slot, 8 + ((slot + 7) & 7))


def kernel(
    n_row,
    n_col,
    grid_hbm,
    noise_ref,
    obs_ref,
    site_noise_ref,
    offset_ref,
    cell_ref,
    count_ref,
    cov_ref,
    first_hbm,
    second_hbm,
    site_out,
    coef_out,
    grid,
    merged,
    mixed,
    smooth,
    first,
    second,
    slots,
    pack,
    row_halo,
    col_halo,
    row_sums,
    col_sums,
    cov_time,
    cov_side,
    band_row,
    band_col,
    band_halo,
    halo_rows,
    spread,
    gather,
    order,
    site_row,
    site_along,
    site_value,
    site_first,
    site_image,
    site_extra,
    sampled,
    list_vmem,
    lists,
    local_sem,
    list_sem,
    send_sem,
    recv_sem,
    row_send,
    row_recv,
    col_send,
    col_recv,
):
    me_row = lax.axis_index("row")
    me_col = lax.axis_index("col")

    load = pltpu.make_async_copy(grid_hbm, grid, local_sem.at[0])
    load.start()

    barrier = pltpu.get_barrier_semaphore()
    for step in range(1, n_row):
        pl.semaphore_signal(
            barrier, inc=1, device_id=(lax.rem(me_row + step, n_row), me_col), device_id_type=MESH
        )
    for step in range(1, n_col):
        pl.semaphore_signal(
            barrier, inc=1, device_id=(me_row, lax.rem(me_col + step, n_col)), device_id_type=MESH
        )

    def exists(down, right):
        row, col = me_row + down, me_col + right
        return (row >= 0) & (row < n_row) & (col >= 0) & (col < n_col)

    diagonals = [(-1, -1), (-1, 1), (1, -1), (1, 1)]
    for down, right in diagonals:

        @pl.when(exists(down, right))
        def _():
            pl.semaphore_signal(
                barrier, inc=1, device_id=(me_row + down, me_col + right), device_id_type=MESH
            )

    @pl.when(me_row == 0)
    def _():
        row_halo[:, 0] = jnp.zeros((2, STEPS, 8, CY), f32)
        col_halo[:, :, :, 0:8, :] = jnp.zeros((2, 2, 2, 8, CY), f32)

    @pl.when(me_row == n_row - 1)
    def _():
        row_halo[:, 1] = jnp.zeros((2, STEPS, 8, CY), f32)
        col_halo[:, :, :, HIGH - 8 : HIGH, :] = jnp.zeros((2, 2, 2, 8, CY), f32)

    @pl.when(me_col == 0)
    def _():
        col_halo[:, 0] = jnp.zeros((2, 2, HIGH, CY), f32)

    @pl.when(me_col == n_col - 1)
    def _():
        col_halo[:, 1] = jnp.zeros((2, 2, HIGH, CY), f32)

    slots[ZERO] = jnp.zeros((CX, CY), f32)

    cell = cell_ref[...]
    row_of = cell >> 7
    key = row_of * SLOT + iota((1, SLOT), 1)
    counts = [jnp.zeros((1, CHUNK), i32) for _ in range(CHUNKS)]
    for j in range(CHUNKS):
        own = jnp.broadcast_to(key[:, j * CHUNK : (j + 1) * CHUNK], (CHUNK, CHUNK)).T
        for k in range(CHUNKS):
            less = own < key[:, k * CHUNK : (k + 1) * CHUNK]
            counts[k] = counts[k] + jnp.sum(jnp.where(less, 1, 0), axis=0, keepdims=True)
    rank = jnp.concatenate(counts, axis=1)
    for j in range(CHUNKS):
        place = iota((CHUNK, SLOT), 0) + j * CHUNK
        order[j * CHUNK : (j + 1) * CHUNK, :] = jnp.where(place == rank, 1.0, 0.0).astype(bf16)

    lead = iota((CHUNKS, SLOT), 0) * CHUNK
    ranks = jnp.broadcast_to(rank, (CHUNKS, SLOT))
    rows_of = jnp.broadcast_to(row_of, (CHUNKS, SLOT))
    lowest = jnp.min(jnp.where(ranks >= lead, rows_of, CX), axis=1, keepdims=True) >> 3
    highest = (jnp.max(jnp.where(ranks < lead + CHUNK, rows_of, 0), axis=1, keepdims=True) + 1) >> 3
    low = [lowest[j : j + 1, :] for j in range(CHUNKS)]
    top = [highest[j : j + 1, :] for j in range(CHUNKS)]
    begin = [jnp.zeros((1, 1), i32)]
    for j in range(CHUNKS):
        begin.append(begin[j] + top[j] - low[j] + 1)
    lane = iota((1, CHUNK), 1)
    one, none = jnp.ones((1, CHUNK), i32), jnp.zeros((1, CHUNK), i32)
    chunk_of = none
    for j in range(1, CHUNKS):
        chunk_of = chunk_of + jnp.where(begin[j] <= lane, one, none)

    def choose(which, values):
        result = jnp.broadcast_to(values[0], (1, CHUNK))
        for j in range(1, CHUNKS):
            result = jnp.where(which == j, values[j], result)
        return result

    start_of = choose(chunk_of, begin)
    group_of = jnp.minimum(choose(chunk_of, low) + lane - start_of, GROUPS - 1)
    blank = jnp.full((1, 1), -1, i32)
    link = choose(chunk_of, [blank] + begin[: CHUNKS - 1]) + group_of
    link = link - choose(chunk_of, [blank] + low[:-1])
    link = jnp.where(group_of <= choose(chunk_of, [blank] + top[:-1]), link, ZERO)
    last = none - 1
    for j in range(CHUNKS):
        last = last + jnp.where(low[j] <= lane, one, none)
    final = choose(last, begin) + lane - choose(last, low)
    final = jnp.where((last >= 0) & (choose(last, top) >= lane), final, ZERO)
    ends = none
    for j in range(CHUNKS):
        ends = jnp.where(lane == j, begin[j + 1] - 1, ends)
    listed = [chunk_of, group_of, link, jnp.where(lane == start_of, ZERO, lane - 1), final, ends]
    for row, values in enumerate(listed):
        list_vmem[row : row + 1, :] = jnp.clip(values, 0, ZERO)
    list_vmem[6:8, :] = jnp.zeros((2, CHUNK), i32)
    listing = pltpu.make_async_copy(list_vmem, lists, list_sem)
    listing.start()

    live = jnp.where(iota((1, SLOT), 1) < count_ref[...], 1.0, 0.0)
    carried = jnp.concatenate(
        [
            live * obs_ref[...],
            offset_ref[...],
            site_noise_ref[...],
            live,
            row_of.astype(f32),
            (cell & (CY - 1)).astype(f32),
            jnp.zeros((10, SLOT), f32),
        ],
        axis=0,
    )
    placed = dot_nt(three(carried), order[...])
    placed = placed[0:48] + placed[48:96] + placed[96:144]
    site_first[...] = placed[0:STEPS]
    site_extra[...] = placed[STEPS : STEPS + 8]
    zeros = jnp.zeros((CHUNK, CHUNK), bf16)
    for j in range(CHUNKS):
        here = slice(j * CHUNK, (j + 1) * CHUNK)
        along_row, along_col = placed[32:33, here], placed[33:34, here]
        row, col = placed[36:37, here].astype(i32), placed[37:38, here].astype(i32)
        site_row[j] = jnp.broadcast_to(row, (8, CHUNK))
        site_along[j] = jnp.broadcast_to(along_row, (8, CHUNK))
        column = iota((CY, CHUNK), 0)
        weight = jnp.where(column == col, 1.0 - along_col, 0.0)
        weight = weight + jnp.where(column == col + 1, along_col, 0.0)
        high, rest = split(weight)
        spread[j, 0:CY, :] = jnp.concatenate([high, high], axis=1)
        spread[j, CY : 2 * CY, :] = jnp.concatenate([rest, zeros], axis=1)
        gather[j, 0:CY, :] = jnp.concatenate([high, rest], axis=1)
        gather[j, CY : 2 * CY, :] = jnp.concatenate([high, zeros], axis=1)
    site_live = site_extra[3:4, :]
    site_noise = site_extra[2:3, :]

    cov_high, cov_rest = split(cov_ref[...])
    eights = [
        lambda x: x >> 3,
        functools.partial(lane_step, side=0),
        functools.partial(lane_step, side=1),
    ]
    same = (iota((2 * CY, 2 * CY), 0) & 7) == (iota((2 * CY, 2 * CY), 1) & 7)
    for kind, step_of in enumerate(eights):
        tall = jnp.where(step_of(iota((2 * CY, STEPS), 0)) == iota((2 * CY, STEPS), 1), 1.0, 0.0)
        wide = jnp.where(step_of(iota((STEPS, 2 * CY), 1)) == iota((STEPS, 2 * CY), 0), 1.0, 0.0)
        tall, wide = tall.astype(bf16), wide.astype(bf16)
        for part, values in enumerate((cov_high, cov_rest)):
            block = dot(tall, dot(values, wide).astype(bf16))
            block = jnp.where(same, block, 0.0).astype(bf16)
            if kind == 0:
                cov_time[part] = block
            else:
                cov_side[kind - 1, part] = block
    high, rest = split(taper(iota((CHUNK, CHUNK + 16), 1) - 8 - iota((CHUNK, CHUNK + 16), 0)))
    band_row[0:CHUNK] = high
    band_row[CHUNK : 2 * CHUNK] = rest

    def quad(ref, weight):
        high, rest = split(weight)
        ref[0:CY, :] = jnp.concatenate([high, rest], axis=1)
        ref[CY : 2 * CY, :] = jnp.concatenate([high, jnp.zeros_like(high)], axis=1)

    line, column = iota((CY, CY), 0), iota((CY, CY), 1)
    quad(band_col, taper(line - column))
    from_left = taper(column + 8 - (line & 7))
    from_right = taper(CY + (line & 7) - column)

    def fill_halo(index, _):
        left = 2 * (index & 7) + (index >> 3)
        right = (left + 1) & 15
        place = line >> 3
        weight = jnp.where(place == left, from_left, 0.0)
        weight = weight + jnp.where(place == right, from_right, 0.0)
        quad(band_halo.at[index], weight)
        return 0

    lax.fori_loop(0, 16, fill_halo, 0)

    listing.wait()
    load.wait()

    signals = (n_row - 1) + (n_col - 1)
    for down, right in diagonals:
        signals = signals + jnp.where(exists(down, right), 1, 0)
    pl.semaphore_wait(barrier, signals)

    def row_weight(chunk, group):
        row = site_row[chunk] - 8 * group
        along = site_along[chunk]
        line = iota((8, CHUNK), 0)
        return jnp.where(row == line, 1.0 - along, 0.0) + jnp.where(row + 1 == line, along, 0.0)

    def messages(call):
        table = [
            (-1, 0, merged.at[:, 0:8, :], row_halo.at[call, 1]),
            (1, 0, merged.at[:, CX - 8 : CX, :], row_halo.at[call, 0]),
            (0, 1, pack.at[0], col_halo.at[call, 0, :, 8 : 8 + CX, :]),
            (0, -1, pack.at[1], col_halo.at[call, 1, :, 8 : 8 + CX, :]),
            (-1, 1, pack.at[0, :, 0:8, :], col_halo.at[call, 0, :, HIGH - 8 : HIGH, :]),
            (1, 1, pack.at[0, :, CX - 8 : CX, :], col_halo.at[call, 0, :, 0:8, :]),
            (-1, -1, pack.at[1, :, 0:8, :], col_halo.at[call, 1, :, HIGH - 8 : HIGH, :]),
            (1, -1, pack.at[1, :, CX - 8 : CX, :], col_halo.at[call, 1, :, 0:8, :]),
        ]
        return [
            (
                down,
                right,
                pltpu.make_async_remote_copy(
                    src_ref=source,
                    dst_ref=target,
                    send_sem=send_sem.at[call, index],
                    recv_sem=recv_sem.at[call, index],
                    device_id=(me_row + down, me_col + right),
                    device_id_type=MESH,
                ),
            )
            for index, (down, right, source, target) in enumerate(table)
        ]

    def mix(values):
        rhs = both(values)
        return halves(dot(cov_time[0], rhs)) + dot(cov_time[1], rhs[:, :CY])

    def sweep_rows(values):
        result = dot(band_row[...], both(values))
        return halves(result[0:CHUNK]) + result[CHUNK : 2 * CHUNK, 0:CY]

    def sum_start(call, tile):
        row_sums[call, pl.ds(me_row, 1)] = tile[None]
        copies = []
        for step in range(1, n_row):
            copy = pltpu.make_async_remote_copy(
                src_ref=row_sums.at[call, me_row],
                dst_ref=row_sums.at[call, me_row],
                send_sem=row_send.at[call, step],
                recv_sem=row_recv.at[call, step],
                device_id=(lax.rem(me_row + step, n_row), me_col),
                device_id_type=MESH,
            )
            copy.start()
            copies.append(copy)
        return copies

    def sum_cross(call, copies):
        for copy in copies:
            copy.wait()
        tile = row_sums[call, 0]
        for index in range(1, n_row):
            tile = tile + row_sums[call, index]
        col_sums[call, pl.ds(me_col, 1)] = tile[None]
        copies = []
        for step in range(1, n_col):
            copy = pltpu.make_async_remote_copy(
                src_ref=col_sums.at[call, me_col],
                dst_ref=col_sums.at[call, me_col],
                send_sem=col_send.at[call, step],
                recv_sem=col_recv.at[call, step],
                device_id=(me_row, lax.rem(me_col + step, n_col)),
                device_id_type=MESH,
            )
            copy.start()
            copies.append(copy)
        return copies

    def sum_end(call, copies):
        for copy in copies:
            copy.wait()
        tile = col_sums[call, 0]
        for index in range(1, n_col):
            tile = tile + col_sums[call, index]
        return jnp.sum(tile, axis=1, keepdims=True)

    def tile_of(parts):
        rows = [jnp.sum(part, axis=0, keepdims=True) for part in parts]
        rows.append(jnp.zeros((8 - len(parts), CY), f32))
        return jnp.concatenate(rows, axis=0)

    def operate(call, source, sites, target, before_sweep, finish):
        values = sites * site_live
        for j in range(CHUNKS):
            part = values[:, j * CHUNK : (j + 1) * CHUNK]
            site_value[j] = jnp.broadcast_to(part[:, None, :], (STEPS, 8, CHUNK))

        def scatter(pair, _):
            chunk, group, link = lists[0, pair], lists[1, pair], lists[2, pair]
            value = site_value[chunk] * row_weight(chunk, group)[None]
            result = dot_nt(both(value.reshape(CX, CHUNK)), spread[chunk])
            slots[pair] = halves(result) + slots[link]
            return 0

        lax.fori_loop(0, PAIRS, scatter, 0)

        def join(group, _):
            here = pl.ds(pl.multiple_of(8 * group, 8), 8)
            values = source[:, here, :] + slots[lists[4, group]].reshape(STEPS, 8, CY)
            merged[:, here, :] = values
            place = iota((8, CY), 1) >> 3
            for pair in range(2):
                ahead = jnp.zeros((8, CY), f32)
                behind = jnp.zeros((8, CY), f32)
                for step in range(16):
                    slot = 2 * (step & 7) + (step >> 3)
                    beside = (slot + 1) & 15
                    rolled = values[16 * pair + step]
                    if beside:
                        rolled = pltpu.roll(rolled, 8 * beside, 1)
                    ahead = jnp.where(place == slot, rolled, ahead)
                    behind = jnp.where(place == beside, rolled, behind)
                pack[0, pair, here, :] = ahead
                pack[1, pair, here, :] = behind
            return 0

        lax.fori_loop(0, GROUPS, join, 0)

        halo = messages(call)
        for down, right, copy in halo:

            @pl.when(exists(down, right))
            def _():
                copy.start()

        def temporal(group, _):
            here = pl.ds(pl.multiple_of(8 * group, 8), 8)
            values = mix(merged[:, here, :].reshape(CX, CY))
            there = pl.ds(pl.multiple_of(8 * group + 8, 8), 8)
            mixed[0:STEPS, there, :] = values.reshape(STEPS, 8, CY)
            return 0

        lax.fori_loop(0, GROUPS, temporal, 0)

        for down, right, copy in halo:

            @pl.when(exists(down, right))
            def _():
                copy.wait_send()

            @pl.when(exists(-down, -right))
            def _():
                copy.wait_recv()

        for side, first_row in ((0, 0), (1, HIGH - 8)):
            values = mix(row_halo[call, side].reshape(CX, CY))
            mixed[0:STEPS, first_row : first_row + 8, :] = values.reshape(STEPS, 8, CY)
        sides = []
        for side in range(2):
            values = jnp.concatenate([col_halo[call, side, 0], col_halo[call, side, 1]], axis=1)
            high, rest = split(values)
            weight = cov_side[side, 0]
            sides.append(dot(high, weight) + dot(rest, weight) + dot(high, cov_side[side, 1]))
        even = ((iota((HIGH, CY), 1) >> 3) & 1) == 0
        for pair in range(2):
            left = sides[0][:, pair * CY : (pair + 1) * CY]
            right = sides[1][:, pair * CY : (pair + 1) * CY]
            mixed[STEPS + 2 * pair] = jnp.where(even, left, right)
            mixed[STEPS + 2 * pair + 1] = jnp.where(even, right, left)
        for index in range(4):
            for block in range(2):
                rows = slice(block * CHUNK, (block + 1) * CHUNK)
                window = slice(block * CHUNK, block * CHUNK + CHUNK + 16)
                halo_rows[index, rows, :] = both(sweep_rows(mixed[STEPS + index, window, :]))

        extra = before_sweep()

        def sweep(step, sums):
            for block in range(2):
                rows = slice(block * CHUNK, (block + 1) * CHUNK)
                window = slice(block * CHUNK, block * CHUNK + CHUNK + 16)
                swept = both(sweep_rows(mixed[step, window, :]))
                result = dot(swept, band_col[...])
                result = result + dot(halo_rows[step >> 3, rows, :], band_halo[step & 15])
                field = halves(result)
                smooth[16 * block : 16 * block + 16, step] = field.reshape(16, 8, CY)
                image = 0.25 * field + noise_ref[rows, :] * source[step, rows, :]
                target[step, rows, :] = image
                terms = finish(extra, grid[step, rows, :], first[step, rows, :], image)
                sums = tuple(total + fold(term) for total, term in zip(sums, terms))
            return sums

        width = 2 if call == 0 else 4
        sums = lax.fori_loop(0, STEPS, sweep, (jnp.zeros((8, CY), f32),) * width)

        def collect(pair, _):
            chunk, group, link = lists[0, pair], lists[1, pair], lists[3, pair]
            values = both(smooth[group].reshape(CX, CY))
            result = halves(dot(values, gather[chunk])).reshape(STEPS, 8, CHUNK)
            result = result * row_weight(chunk, group)[None]
            slots[pair] = result.reshape(CX, CHUNK) + slots[link]
            return 0

        lax.fori_loop(0, PAIRS, collect, 0)
        for j in range(CHUNKS):
            total = slots[lists[5, j]].reshape(STEPS, 8, CHUNK)
            sampled[:, j * CHUNK : (j + 1) * CHUNK] = jnp.sum(total, axis=1)
        image = site_live * (0.25 * sampled[...] + site_noise * sites) + (1.0 - site_live) * sites
        terms = finish(extra, site_first[...], site_image[...], image)
        return [total + fold(term) for total, term in zip(sums, terms)], image

    def first_terms(extra, start, seen, image):
        return start * start, start * image

    sums, image = operate(0, grid, site_first[...], first, lambda: None, first_terms)
    site_image[...] = image
    save_first = pltpu.make_async_copy(first, first_hbm, local_sem.at[1])
    save_first.start()
    pending = sum_start(0, tile_of(sums))

    def step_length():
        total = sum_end(0, sum_cross(0, pending))
        return total[0:1], total[1:2]

    kept = []

    def before_sweep():
        norm, across = step_length()
        kept.extend([norm, across])
        return norm / across

    def second_terms(alpha, start, image, twice):
        residual = start - alpha * image
        applied = image - alpha * twice
        return residual * residual, residual * applied, residual * image, start * applied

    sums, _ = operate(1, first, site_image[...], second, before_sweep, second_terms)
    save_second = pltpu.make_async_copy(second, second_hbm, local_sem.at[2])
    save_second.start()
    pending = sum_start(1, tile_of(sums))
    restored = dot(three(site_image[...]), order[...])
    site_out[...] = restored[0:STEPS] + restored[STEPS : 2 * STEPS] + restored[2 * STEPS :]
    total = sum_end(1, sum_cross(1, pending))
    norm, across = kept
    alpha = norm / across
    after = total[0:1]
    beta = after / norm
    curve = total[1:2] + beta * (total[2:3] + total[3:4]) + beta * beta * across
    alpha_next = after / curve
    line = iota((8, CY), 0)
    direct = alpha + alpha_next * (1.0 + beta)
    cross = -(alpha * alpha_next)
    coef_out[...] = jnp.where(line == 0, direct, cross)
    save_first.wait()
    save_second.wait()


def body(
    n_row,
    n_col,
    grid_obs,
    grid_noise,
    station_obs,
    station_noise,
    station_offset,
    station_cell,
    station_count,
    time_cov,
):
    vmem = pl.BlockSpec(memory_space=pltpu.VMEM)
    anywhere = pl.BlockSpec(memory_space=pl.ANY)
    field = (STEPS, CX, CY)
    sites = station_obs.reshape(STEPS, SLOT)
    dma = pltpu.SemaphoreType.DMA
    first, second, site_image, coef = pl.pallas_call(
        functools.partial(kernel, n_row, n_col),
        out_shape=(
            jax.ShapeDtypeStruct(field, f32),
            jax.ShapeDtypeStruct(field, f32),
            jax.ShapeDtypeStruct((STEPS, SLOT), f32),
            jax.ShapeDtypeStruct((8, CY), f32),
        ),
        in_specs=[anywhere] + [vmem] * 7,
        out_specs=(anywhere, anywhere, vmem, vmem),
        scratch_shapes=[
            pltpu.VMEM(field, f32),
            pltpu.VMEM(field, f32),
            pltpu.VMEM((STEPS + 4, HIGH, CY), f32),
            pltpu.VMEM((GROUPS, STEPS, 8, CY), f32),
            pltpu.VMEM(field, f32),
            pltpu.VMEM(field, f32),
            pltpu.VMEM((ZERO + 1, CX, CY), f32),
            pltpu.VMEM((2, 2, CX, CY), f32),
            pltpu.VMEM((2, 2, STEPS, 8, CY), f32),
            pltpu.VMEM((2, 2, 2, HIGH, CY), f32),
            pltpu.VMEM((2, n_row, 8, CY), f32),
            pltpu.VMEM((2, n_col, 8, CY), f32),
            pltpu.VMEM((2, 2 * CY, 2 * CY), bf16),
            pltpu.VMEM((2, 2, 2 * CY, 2 * CY), bf16),
            pltpu.VMEM((2 * CHUNK, CHUNK + 16), bf16),
            pltpu.VMEM((2 * CY, 2 * CY), bf16),
            pltpu.VMEM((16, 2 * CY, 2 * CY), bf16),
            pltpu.VMEM((4, CX, 2 * CY), bf16),
            pltpu.VMEM((CHUNKS, 2 * CY, 2 * CHUNK), bf16),
            pltpu.VMEM((CHUNKS, 2 * CY, 2 * CHUNK), bf16),
            pltpu.VMEM((SLOT, SLOT), bf16),
            pltpu.VMEM((CHUNKS, 8, CHUNK), i32),
            pltpu.VMEM((CHUNKS, 8, CHUNK), f32),
            pltpu.VMEM((CHUNKS, STEPS, 8, CHUNK), f32),
            pltpu.VMEM((STEPS, SLOT), f32),
            pltpu.VMEM((STEPS, SLOT), f32),
            pltpu.VMEM((8, SLOT), f32),
            pltpu.VMEM((STEPS, SLOT), f32),
            pltpu.VMEM((8, CHUNK), i32),
            pltpu.SMEM((8, CHUNK), i32),
            dma((3,)),
            dma,
            dma((2, 8)),
            dma((2, 8)),
            dma((2, n_row)),
            dma((2, n_row)),
            dma((2, n_col)),
            dma((2, n_col)),
        ],
        compiler_params=pltpu.CompilerParams(
            collective_id=0, has_side_effects=True, vmem_limit_bytes=58 * 2**20
        ),
        name="kriging",
    )(
        grid_obs,
        grid_noise,
        sites,
        station_noise.reshape(1, SLOT),
        station_offset.reshape(2, SLOT),
        station_cell.reshape(1, SLOT),
        station_count,
        time_cov,
    )
    direct, cross = coef[0, 0], coef[1, 0]
    live = (jnp.arange(SLOT, dtype=i32)[None, :] < station_count).astype(f32)
    solution_grid = direct * grid_obs + cross * first
    residual_grid = grid_obs - direct * first - cross * second
    solution_sites = direct * (live * sites) + cross * site_image
    return solution_grid, solution_sites.reshape(STEPS, 1, 1, SLOT), residual_grid


def solution(mesh):
    placed = (
        P(None, "row", "col"),
        P("row", "col"),
        P(None, "row", "col", None),
        P("row", "col", None),
        P(None, "row", "col", None),
        P("row", "col", None),
        P("row", "col"),
        P(),
    )
    return jax.shard_map(
        functools.partial(body, mesh.shape["row"], mesh.shape["col"]),
        mesh=mesh,
        in_specs=placed,
        out_specs=(P(None, "row", "col"), P(None, "row", "col", None), P(None, "row", "col")),
        check_vma=False,
    )
```

```python
import functools

import jax
import jax.numpy as jnp
from jax import lax
from jax.experimental import pallas as pl
from jax.experimental.pallas import tpu as pltpu
from jax.sharding import PartitionSpec as P

REACH = 8
CLOSE = 8
CX = 256
CY = 128
STEPS = 32
SLOT = 1024
CHUNK = 128
CHUNKS = SLOT // CHUNK
GROUPS = CX // 8
PAIRS = GROUPS + 2 * CHUNKS
ZERO = PAIRS
HIGH = CX + 2 * REACH
MESH = pl.DeviceIdType.MESH
f32, bf16, i32 = jnp.float32, jnp.bfloat16, jnp.int32


def iota(shape, dim):
    return lax.broadcasted_iota(i32, shape, dim)


def taper(offset):
    distance = jnp.abs(offset)
    spread = distance.astype(f32)
    value = (1.0 - spread / (REACH + 1)) * jnp.exp(-spread / 3.0)
    return jnp.where(distance <= REACH, value, 0.0)


def split(x):
    high = x.astype(bf16)
    return high, (x - high.astype(f32)).astype(bf16)


def both(x):
    return jnp.concatenate(split(x), axis=1)


def three(x):
    high = x.astype(bf16)
    rest = x - high.astype(f32)
    middle = rest.astype(bf16)
    return jnp.concatenate([high, middle, (rest - middle.astype(f32)).astype(bf16)], axis=0)


def dot(a, b):
    return lax.dot_general(a, b, (((1,), (0,)), ((), ())), preferred_element_type=f32)


def dot_nt(a, b):
    return lax.dot_general(a, b, (((1,), (1,)), ((), ())), preferred_element_type=f32)


def quad(ref, weight):
    high, rest = split(weight)
    ref[0:CY, :] = jnp.concatenate([high, rest], axis=1)
    ref[CY : 2 * CY, :] = jnp.concatenate([high, jnp.zeros_like(high)], axis=1)


def halves(x):
    return x[:, :CY] + x[:, CY:]


def fold(x):
    rows, cols = x.shape
    total = jnp.zeros((8, CY), f32)
    for c in range(cols // CY):
        total = total + jnp.sum(x[:, c * CY : (c + 1) * CY].reshape(rows // 8, 8, CY), axis=0)
    return total


def lane_step(lane, side):
    pair = lane >> 7
    place = (lane >> 3) & 15
    slot, odd = place >> 1, place & 1
    if side == 0:
        return 16 * pair + 8 * odd + slot
    return 16 * pair + jnp.where(odd == 1, slot, 8 + ((slot + 7) & 7))


def kernel(
    n_row,
    n_col,
    grid_hbm,
    noise_ref,
    obs_hbm,
    site_noise_ref,
    offset_hbm,
    cell_ref,
    count_ref,
    cov_ref,
    first,
    second,
    start_out,
    site_out,
    coef_out,
    grid,
    merged,
    mixed,
    smooth,
    obs_ref,
    offset_ref,
    slots,
    pack,
    row_halo,
    col_halo,
    row_sums,
    col_sums,
    cov_time,
    cov_side,
    band_row,
    band_col,
    halo_rows,
    spread,
    gather,
    order,
    site_row,
    site_along,
    site_value,
    site_first,
    site_image,
    site_extra,
    sampled,
    list_vmem,
    lists,
    local_sem,
    list_sem,
    send_sem,
    recv_sem,
    row_send,
    row_recv,
    col_send,
    col_recv,
):
    me_row = lax.axis_index("row")
    me_col = lax.axis_index("col")

    loads = [
        pltpu.make_async_copy(obs_hbm.at[step, 0], obs_ref.at[step : step + 1], local_sem.at[step])
        for step in range(STEPS)
    ]
    for part in range(2):
        loads.append(
            pltpu.make_async_copy(
                offset_hbm.at[part, 0],
                offset_ref.at[part : part + 1],
                local_sem.at[STEPS + part],
            )
        )
    for copy in loads:
        copy.start()
    load = pltpu.make_async_copy(grid_hbm, grid, local_sem.at[STEPS + 2])
    load.start()

    barrier = pltpu.get_barrier_semaphore()
    for step in range(1, n_row):
        pl.semaphore_signal(
            barrier, inc=1, device_id=(lax.rem(me_row + step, n_row), me_col), device_id_type=MESH
        )
    for step in range(1, n_col):
        pl.semaphore_signal(
            barrier, inc=1, device_id=(me_row, lax.rem(me_col + step, n_col)), device_id_type=MESH
        )

    def exists(down, right):
        row, col = me_row + down, me_col + right
        return (row >= 0) & (row < n_row) & (col >= 0) & (col < n_col)

    diagonals = [(-1, -1), (-1, 1), (1, -1), (1, 1)]
    for down, right in diagonals:

        @pl.when(exists(down, right))
        def _():
            pl.semaphore_signal(
                barrier, inc=1, device_id=(me_row + down, me_col + right), device_id_type=MESH
            )

    @pl.when(me_row == 0)
    def _():
        row_halo[:, 0] = jnp.zeros((2, STEPS, 8, CY), f32)
        col_halo[:, :, :, 0:8, :] = jnp.zeros((2, 2, 2, 8, CY), f32)

    @pl.when(me_row == n_row - 1)
    def _():
        row_halo[:, 1] = jnp.zeros((2, STEPS, 8, CY), f32)
        col_halo[:, :, :, HIGH - 8 : HIGH, :] = jnp.zeros((2, 2, 2, 8, CY), f32)

    @pl.when(me_col == 0)
    def _():
        col_halo[:, 0] = jnp.zeros((2, 2, HIGH, CY), f32)

    @pl.when(me_col == n_col - 1)
    def _():
        col_halo[:, 1] = jnp.zeros((2, 2, HIGH, CY), f32)

    slots[ZERO] = jnp.zeros((CX, CY), f32)

    cell = cell_ref[...]
    row_of = cell >> 7
    key = row_of * SLOT + iota((1, SLOT), 1)
    counts = [jnp.zeros((1, CHUNK), i32) for _ in range(CHUNKS)]
    for j in range(CHUNKS):
        own = jnp.broadcast_to(key[:, j * CHUNK : (j + 1) * CHUNK], (CHUNK, CHUNK)).T
        for k in range(CHUNKS):
            less = own < key[:, k * CHUNK : (k + 1) * CHUNK]
            counts[k] = counts[k] + jnp.sum(jnp.where(less, 1, 0), axis=0, keepdims=True)
    rank = jnp.concatenate(counts, axis=1)
    for j in range(CHUNKS):
        place = iota((CHUNK, SLOT), 0) + j * CHUNK
        order[j * CHUNK : (j + 1) * CHUNK, :] = jnp.where(place == rank, 1.0, 0.0).astype(bf16)

    lead = iota((CHUNKS, SLOT), 0) * CHUNK
    ranks = jnp.broadcast_to(rank, (CHUNKS, SLOT))
    rows_of = jnp.broadcast_to(row_of, (CHUNKS, SLOT))
    lowest = jnp.min(jnp.where(ranks >= lead, rows_of, CX), axis=1, keepdims=True) >> 3
    highest = (jnp.max(jnp.where(ranks < lead + CHUNK, rows_of, 0), axis=1, keepdims=True) + 1) >> 3
    low = [lowest[j : j + 1, :] for j in range(CHUNKS)]
    top = [highest[j : j + 1, :] for j in range(CHUNKS)]
    begin = [jnp.zeros((1, 1), i32)]
    for j in range(CHUNKS):
        begin.append(begin[j] + top[j] - low[j] + 1)
    lane = iota((1, CHUNK), 1)
    one, none = jnp.ones((1, CHUNK), i32), jnp.zeros((1, CHUNK), i32)
    chunk_of = none
    for j in range(1, CHUNKS):
        chunk_of = chunk_of + jnp.where(begin[j] <= lane, one, none)

    def choose(which, values):
        result = jnp.broadcast_to(values[0], (1, CHUNK))
        for j in range(1, CHUNKS):
            result = jnp.where(which == j, values[j], result)
        return result

    start_of = choose(chunk_of, begin)
    group_of = jnp.minimum(choose(chunk_of, low) + lane - start_of, GROUPS - 1)
    blank = jnp.full((1, 1), -1, i32)
    link = choose(chunk_of, [blank] + begin[: CHUNKS - 1]) + group_of
    link = link - choose(chunk_of, [blank] + low[:-1])
    link = jnp.where(group_of <= choose(chunk_of, [blank] + top[:-1]), link, ZERO)
    last = none - 1
    for j in range(CHUNKS):
        last = last + jnp.where(low[j] <= lane, one, none)
    final = choose(last, begin) + lane - choose(last, low)
    final = jnp.where((last >= 0) & (choose(last, top) >= lane), final, ZERO)
    ends = none
    for j in range(CHUNKS):
        ends = jnp.where(lane == j, begin[j + 1] - 1, ends)
    listed = [chunk_of, group_of, link, jnp.where(lane == start_of, ZERO, lane - 1), final, ends]
    for row, values in enumerate(listed):
        list_vmem[row : row + 1, :] = jnp.clip(values, 0, ZERO)
    list_vmem[6:8, :] = jnp.zeros((2, CHUNK), i32)
    listing = pltpu.make_async_copy(list_vmem, lists, list_sem)
    listing.start()

    for copy in loads:
        copy.wait()
    live = jnp.where(iota((1, SLOT), 1) < count_ref[...], 1.0, 0.0)
    start_out[...] = live * obs_ref[...]
    carried = jnp.concatenate(
        [
            start_out[...],
            offset_ref[...],
            site_noise_ref[...],
            live,
            row_of.astype(f32),
            (cell & (CY - 1)).astype(f32),
            jnp.zeros((10, SLOT), f32),
        ],
        axis=0,
    )
    placed = dot_nt(three(carried), order[...])
    placed = placed[0:48] + placed[48:96] + placed[96:144]
    site_first[...] = placed[0:STEPS]
    site_extra[...] = placed[STEPS : STEPS + 8]
    for j in range(CHUNKS):
        here = slice(j * CHUNK, (j + 1) * CHUNK)
        along_row, along_col = placed[32:33, here], placed[33:34, here]
        row, col = placed[36:37, here].astype(i32), placed[37:38, here].astype(i32)
        site_row[j] = jnp.broadcast_to(row, (8, CHUNK))
        site_along[j] = jnp.broadcast_to(along_row, (8, CHUNK))
        column = iota((CY, CHUNK), 0)
        weight = jnp.where(column == col, 1.0 - along_col, 0.0)
        weight = weight + jnp.where(column == col + 1, along_col, 0.0)
        quad(gather.at[j], weight)
        quad(spread.at[j], weight.T)
    site_live = site_extra[3:4, :]
    site_noise = site_extra[2:3, :]

    cov_high, cov_rest = split(cov_ref[...])
    eights = [
        lambda x: x >> 3,
        functools.partial(lane_step, side=0),
        functools.partial(lane_step, side=1),
    ]
    same = (iota((2 * CY, 2 * CY), 0) & 7) == (iota((2 * CY, 2 * CY), 1) & 7)
    for kind, step_of in enumerate(eights):
        tall = jnp.where(step_of(iota((2 * CY, STEPS), 0)) == iota((2 * CY, STEPS), 1), 1.0, 0.0)
        wide = jnp.where(step_of(iota((STEPS, 2 * CY), 1)) == iota((STEPS, 2 * CY), 0), 1.0, 0.0)
        tall, wide = tall.astype(bf16), wide.astype(bf16)
        for part, values in enumerate((cov_high, cov_rest)):
            block = dot(tall, dot(values, wide).astype(bf16))
            block = jnp.where(same, block, 0.0).astype(bf16)
            if kind == 0:
                cov_time[part] = block
            else:
                cov_side[kind - 1, part] = block
    high, rest = split(taper(iota((CHUNK, CHUNK + 16), 1) - 8 - iota((CHUNK, CHUNK + 16), 0)))
    band_row[0:CHUNK] = high
    band_row[CHUNK : 2 * CHUNK] = rest

    line, column = iota((CY, CY), 0), iota((CY, CY), 1)
    own = taper(line - column)
    from_left = taper(column + 8 - (line & 7))
    from_right = taper(CY + (line & 7) - column)

    def fill_halo(index, _):
        left = 2 * (index & 7) + (index >> 3)
        right = (left + 1) & 15
        place = line >> 3
        weight = jnp.where(place == left, from_left, 0.0)
        weight = weight + jnp.where(place == right, from_right, 0.0)
        quad(band_col.at[index, 0 : 2 * CY], own)
        quad(band_col.at[index, 2 * CY : 4 * CY], weight)
        return 0

    lax.fori_loop(0, 16, fill_halo, 0)

    listing.wait()
    load.wait()

    signals = (n_row - 1) + (n_col - 1)
    for down, right in diagonals:
        signals = signals + jnp.where(exists(down, right), 1, 0)
    pl.semaphore_wait(barrier, signals)

    def row_weight(chunk, group):
        row = site_row[chunk] - 8 * group
        along = site_along[chunk]
        line = iota((8, CHUNK), 0)
        return jnp.where(row == line, 1.0 - along, 0.0) + jnp.where(row + 1 == line, along, 0.0)

    def messages(call):
        table = [
            (-1, 0, merged.at[:, 0:8, :], row_halo.at[call, 1]),
            (1, 0, merged.at[:, CX - 8 : CX, :], row_halo.at[call, 0]),
            (0, 1, pack.at[0], col_halo.at[call, 0, :, 8 : 8 + CX, :]),
            (0, -1, pack.at[1], col_halo.at[call, 1, :, 8 : 8 + CX, :]),
            (-1, 1, pack.at[0, :, 0:8, :], col_halo.at[call, 0, :, HIGH - 8 : HIGH, :]),
            (1, 1, pack.at[0, :, CX - 8 : CX, :], col_halo.at[call, 0, :, 0:8, :]),
            (-1, -1, pack.at[1, :, 0:8, :], col_halo.at[call, 1, :, HIGH - 8 : HIGH, :]),
            (1, -1, pack.at[1, :, CX - 8 : CX, :], col_halo.at[call, 1, :, 0:8, :]),
        ]
        return [
            (
                down,
                right,
                pltpu.make_async_remote_copy(
                    src_ref=source,
                    dst_ref=target,
                    send_sem=send_sem.at[call, index],
                    recv_sem=recv_sem.at[call, index],
                    device_id=(me_row + down, me_col + right),
                    device_id_type=MESH,
                ),
            )
            for index, (down, right, source, target) in enumerate(table)
        ]

    def mix(values):
        rhs = both(values)
        return halves(dot(cov_time[0], rhs)) + dot(cov_time[1], rhs[:, :CY])

    def sweep_rows(values):
        result = dot(band_row[...], both(values))
        return halves(result[0:CHUNK]) + result[CHUNK : 2 * CHUNK, 0:CY]

    def sum_start(call, tile):
        row_sums[call, pl.ds(me_row, 1)] = tile[None]
        copies = []
        for step in range(1, n_row):
            copy = pltpu.make_async_remote_copy(
                src_ref=row_sums.at[call, me_row],
                dst_ref=row_sums.at[call, me_row],
                send_sem=row_send.at[call, step],
                recv_sem=row_recv.at[call, step],
                device_id=(lax.rem(me_row + step, n_row), me_col),
                device_id_type=MESH,
            )
            copy.start()
            copies.append(copy)
        return copies

    def sum_cross(call, copies):
        for copy in copies:
            copy.wait()
        tile = row_sums[call, 0]
        for index in range(1, n_row):
            tile = tile + row_sums[call, index]
        col_sums[call, pl.ds(me_col, 1)] = tile[None]
        copies = []
        for step in range(1, n_col):
            copy = pltpu.make_async_remote_copy(
                src_ref=col_sums.at[call, me_col],
                dst_ref=col_sums.at[call, me_col],
                send_sem=col_send.at[call, step],
                recv_sem=col_recv.at[call, step],
                device_id=(me_row, lax.rem(me_col + step, n_col)),
                device_id_type=MESH,
            )
            copy.start()
            copies.append(copy)
        return copies

    def sum_end(call, copies):
        for copy in copies:
            copy.wait()
        tile = col_sums[call, 0]
        for index in range(1, n_col):
            tile = tile + col_sums[call, index]
        return jnp.sum(tile, axis=1, keepdims=True)

    def tile_of(parts):
        rows = [jnp.sum(part, axis=0, keepdims=True) for part in parts]
        rows.append(jnp.zeros((8 - len(parts), CY), f32))
        return jnp.concatenate(rows, axis=0)

    def operate(call, source, sites, target, before_sweep, finish):
        values = sites * site_live
        for j in range(CHUNKS):
            part = values[:, j * CHUNK : (j + 1) * CHUNK]
            site_value[j] = jnp.broadcast_to(part[:, None, :], (STEPS, 8, CHUNK))

        def scatter(pair, _):
            chunk, group, link = lists[0, pair], lists[1, pair], lists[2, pair]
            value = site_value[chunk] * row_weight(chunk, group)[None]
            result = dot(both(value.reshape(CX, CHUNK)), spread[chunk])
            slots[pair] = halves(result) + slots[link]
            return 0

        lax.fori_loop(0, PAIRS, scatter, 0, unroll=16)

        def join(group, _):
            here = pl.ds(pl.multiple_of(8 * group, 8), 8)
            values = source[:, here, :] + slots[lists[4, group]].reshape(STEPS, 8, CY)
            merged[:, here, :] = values
            place = iota((8, CY), 1) >> 3
            for pair in range(2):
                ahead = jnp.zeros((8, CY), f32)
                behind = jnp.zeros((8, CY), f32)
                for step in range(16):
                    slot = 2 * (step & 7) + (step >> 3)
                    beside = (slot + 1) & 15
                    rolled = values[16 * pair + step]
                    if beside:
                        rolled = pltpu.roll(rolled, 8 * beside, 1)
                    ahead = jnp.where(place == slot, rolled, ahead)
                    behind = jnp.where(place == beside, rolled, behind)
                pack[0, pair, here, :] = ahead
                pack[1, pair, here, :] = behind
            return 0

        lax.fori_loop(0, GROUPS, join, 0, unroll=8)

        halo = messages(call)
        for down, right, copy in halo:

            @pl.when(exists(down, right))
            def _():
                copy.start()

        def temporal(group, _):
            here = pl.ds(pl.multiple_of(8 * group, 8), 8)
            values = mix(merged[:, here, :].reshape(CX, CY))
            there = pl.ds(pl.multiple_of(8 * group + 8, 8), 8)
            mixed[0:STEPS, there, :] = values.reshape(STEPS, 8, CY)
            return 0

        lax.fori_loop(0, GROUPS, temporal, 0, unroll=16)

        for down, right, copy in halo:

            @pl.when(exists(down, right))
            def _():
                copy.wait_send()

            @pl.when(exists(-down, -right))
            def _():
                copy.wait_recv()

        for side, first_row in ((0, 0), (1, HIGH - 8)):
            values = mix(row_halo[call, side].reshape(CX, CY))
            mixed[0:STEPS, first_row : first_row + 8, :] = values.reshape(STEPS, 8, CY)
        sides = []
        for side in range(2):
            values = jnp.concatenate([col_halo[call, side, 0], col_halo[call, side, 1]], axis=1)
            high, rest = split(values)
            weight = cov_side[side, 0]
            sides.append(dot(high, weight) + dot(rest, weight) + dot(high, cov_side[side, 1]))
        even = ((iota((HIGH, CY), 1) >> 3) & 1) == 0
        for pair in range(2):
            left = sides[0][:, pair * CY : (pair + 1) * CY]
            right = sides[1][:, pair * CY : (pair + 1) * CY]
            mixed[STEPS + 2 * pair] = jnp.where(even, left, right)
            mixed[STEPS + 2 * pair + 1] = jnp.where(even, right, left)
        for index in range(4):
            for block in range(2):
                rows = slice(block * CHUNK, (block + 1) * CHUNK)
                window = slice(block * CHUNK, block * CHUNK + CHUNK + 16)
                halo_rows[index, rows, :] = both(sweep_rows(mixed[STEPS + index, window, :]))

        extra = before_sweep()

        def sweep(step, sums):
            swept = [
                both(sweep_rows(mixed[step, block * CHUNK : block * CHUNK + CHUNK + 16, :]))
                for block in range(2)
            ]
            swept = jnp.concatenate(
                [jnp.concatenate(swept, axis=0), halo_rows[step >> 3]], axis=1
            )
            field = halves(dot(swept, band_col[step & 15]))
            smooth[:, step] = field.reshape(GROUPS, 8, CY)
            image = 0.25 * field + noise_ref[...] * source[step]
            target[step] = image
            terms = finish(extra, grid[step], first[step], image)
            sums = tuple(total + fold(term) for total, term in zip(sums, terms))
            return sums

        width = 2 if call == 0 else 4
        sums = lax.fori_loop(0, STEPS, sweep, (jnp.zeros((8, CY), f32),) * width, unroll=16)

        def collect(pair, _):
            chunk, group, link = lists[0, pair], lists[1, pair], lists[3, pair]
            values = both(smooth[group].reshape(CX, CY))
            result = halves(dot(values, gather[chunk])).reshape(STEPS, 8, CHUNK)
            result = result * row_weight(chunk, group)[None]
            slots[pair] = result.reshape(CX, CHUNK) + slots[link]
            return 0

        lax.fori_loop(0, PAIRS, collect, 0, unroll=16)
        for j in range(CHUNKS):
            total = slots[lists[5, j]].reshape(STEPS, 8, CHUNK)
            sampled[:, j * CHUNK : (j + 1) * CHUNK] = jnp.sum(total, axis=1)
        image = site_live * (0.25 * sampled[...] + site_noise * sites) + (1.0 - site_live) * sites
        terms = finish(extra, site_first[...], site_image[...], image)
        return [total + fold(term) for total, term in zip(sums, terms)], image

    def first_terms(extra, start, seen, image):
        return start * start, start * image

    sums, image = operate(0, grid, site_first[...], first, lambda: None, first_terms)
    site_image[...] = image
    pending = sum_start(0, tile_of(sums))

    def step_length():
        total = sum_end(0, sum_cross(0, pending))
        return total[0:1], total[1:2]

    kept = []

    def before_sweep():
        norm, across = step_length()
        kept.extend([norm, across])
        return norm / across

    def second_terms(alpha, start, image, twice):
        residual = start - alpha * image
        applied = image - alpha * twice
        return residual * residual, residual * applied, residual * image, start * applied

    sums, _ = operate(1, first, site_image[...], second, before_sweep, second_terms)
    pending = sum_start(1, tile_of(sums))
    restored = dot(three(site_image[...]), order[...])
    site_out[...] = restored[0:STEPS] + restored[STEPS : 2 * STEPS] + restored[2 * STEPS :]
    total = sum_end(1, sum_cross(1, pending))
    norm, across = kept
    alpha = norm / across
    after = total[0:1]
    beta = after / norm
    curve = total[1:2] + beta * (total[2:3] + total[3:4]) + beta * beta * across
    alpha_next = after / curve
    line = iota((8, CY), 0)
    direct = alpha + alpha_next * (1.0 + beta)
    cross = -(alpha * alpha_next)
    coef_out[...] = jnp.where(line == 0, direct, cross)


def close_kernel(
    coef_ref, first, second, start, image, grid_ref, solution_ref, residual_ref, sites_hbm, sites, sems
):
    index = pl.program_id(0)
    direct, cross = coef_ref[0:1, 0:1], coef_ref[1:2, 0:1]
    copies = [
        pltpu.make_async_copy(sites.at[step : step + 1], sites_hbm.at[step, 0], sems.at[step])
        for step in range(STEPS)
    ]

    @pl.when(index == 0)
    def _():
        sites[...] = direct * start[...] + cross * image[...]
        for copy in copies:
            copy.start()

    count = grid_ref.shape[0]
    for step in range(count):
        own = grid_ref[step]
        once = first[index * count + step]
        twice = second[index * count + step]
        solution_ref[step] = direct * own + cross * once
        residual_ref[step] = own - direct * once - cross * twice

    @pl.when(index == pl.num_programs(0) - 1)
    def _():
        for copy in copies:
            copy.wait()


def body(
    n_row,
    n_col,
    grid_obs,
    grid_noise,
    station_obs,
    station_noise,
    station_offset,
    station_cell,
    station_count,
    time_cov,
):
    vmem = pl.BlockSpec(memory_space=pltpu.VMEM)
    anywhere = pl.BlockSpec(memory_space=pl.ANY)
    field = (STEPS, CX, CY)
    dma = pltpu.SemaphoreType.DMA
    first, second, start, image, coef = pl.pallas_call(
        functools.partial(kernel, n_row, n_col),
        out_shape=(
            pltpu.VMEM(field, f32),
            pltpu.VMEM(field, f32),
            pltpu.VMEM((STEPS, SLOT), f32),
            pltpu.VMEM((STEPS, SLOT), f32),
            pltpu.VMEM((8, CY), f32),
        ),
        in_specs=[anywhere, vmem, anywhere, vmem, anywhere, vmem, vmem, vmem],
        out_specs=(vmem,) * 5,
        scratch_shapes=[
            pltpu.VMEM(field, f32),
            pltpu.VMEM(field, f32),
            pltpu.VMEM((STEPS + 4, HIGH, CY), f32),
            pltpu.VMEM((GROUPS, STEPS, 8, CY), f32),
            pltpu.VMEM((STEPS, SLOT), f32),
            pltpu.VMEM((2, SLOT), f32),
            pltpu.VMEM((ZERO + 1, CX, CY), f32),
            pltpu.VMEM((2, 2, CX, CY), f32),
            pltpu.VMEM((2, 2, STEPS, 8, CY), f32),
            pltpu.VMEM((2, 2, 2, HIGH, CY), f32),
            pltpu.VMEM((2, n_row, 8, CY), f32),
            pltpu.VMEM((2, n_col, 8, CY), f32),
            pltpu.VMEM((2, 2 * CY, 2 * CY), bf16),
            pltpu.VMEM((2, 2, 2 * CY, 2 * CY), bf16),
            pltpu.VMEM((2 * CHUNK, CHUNK + 16), bf16),
            pltpu.VMEM((16, 4 * CY, 2 * CY), bf16),
            pltpu.VMEM((4, CX, 2 * CY), bf16),
            pltpu.VMEM((CHUNKS, 2 * CY, 2 * CHUNK), bf16),
            pltpu.VMEM((CHUNKS, 2 * CY, 2 * CHUNK), bf16),
            pltpu.VMEM((SLOT, SLOT), bf16),
            pltpu.VMEM((CHUNKS, 8, CHUNK), i32),
            pltpu.VMEM((CHUNKS, 8, CHUNK), f32),
            pltpu.VMEM((CHUNKS, STEPS, 8, CHUNK), f32),
            pltpu.VMEM((STEPS, SLOT), f32),
            pltpu.VMEM((STEPS, SLOT), f32),
            pltpu.VMEM((8, SLOT), f32),
            pltpu.VMEM((STEPS, SLOT), f32),
            pltpu.VMEM((8, CHUNK), i32),
            pltpu.SMEM((8, CHUNK), i32),
            dma((STEPS + 3,)),
            dma,
            dma((2, 8)),
            dma((2, 8)),
            dma((2, n_row)),
            dma((2, n_row)),
            dma((2, n_col)),
            dma((2, n_col)),
        ],
        compiler_params=pltpu.CompilerParams(
            collective_id=0, has_side_effects=True, vmem_limit_bytes=48 * 2**20
        ),
        name="kriging",
    )(
        grid_obs,
        grid_noise,
        station_obs,
        station_noise.reshape(1, SLOT),
        station_offset,
        station_cell.reshape(1, SLOT),
        station_count,
        time_cov,
    )
    block = pl.BlockSpec((CLOSE, CX, CY), lambda index: (index, 0, 0))
    solution_grid, residual_grid, solution_sites = pl.pallas_call(
        close_kernel,
        grid=(STEPS // CLOSE,),
        out_shape=(
            jax.ShapeDtypeStruct(field, f32),
            jax.ShapeDtypeStruct(field, f32),
            jax.ShapeDtypeStruct((STEPS, 1, 1, SLOT), f32),
        ),
        in_specs=[vmem] * 5 + [block],
        out_specs=(block, block, anywhere),
        scratch_shapes=[pltpu.VMEM((STEPS, SLOT), f32), dma((STEPS,))],
        compiler_params=pltpu.CompilerParams(vmem_limit_bytes=16 * 2**20),
        name="close",
    )(coef, first, second, start, image, grid_obs)
    return solution_grid, solution_sites, residual_grid


def solution(mesh):
    placed = (
        P(None, "row", "col"),
        P("row", "col"),
        P(None, "row", "col", None),
        P("row", "col", None),
        P(None, "row", "col", None),
        P("row", "col", None),
        P("row", "col"),
        P(),
    )
    return jax.shard_map(
        functools.partial(body, mesh.shape["row"], mesh.shape["col"]),
        mesh=mesh,
        in_specs=placed,
        out_specs=(P(None, "row", "col"), P(None, "row", "col", None), P(None, "row", "col")),
        check_vma=False,
    )
```

```python
import functools

import jax
import jax.numpy as jnp
from jax import lax
from jax.experimental import pallas as pl
from jax.experimental.pallas import tpu as pltpu
from jax.sharding import PartitionSpec as P

REACH = 8
CLOSE = 8
CX = 256
CY = 128
STEPS = 32
SLOT = 1024
CHUNK = 128
CHUNKS = SLOT // CHUNK
GROUPS = CX // 8
PARTS = 4
PART = CX // PARTS
PAIRS = GROUPS + 2 * CHUNKS
ZERO = PAIRS
HIGH = CX + 2 * REACH
MESH = pl.DeviceIdType.MESH
f32, bf16, i32 = jnp.float32, jnp.bfloat16, jnp.int32


def iota(shape, dim):
    return lax.broadcasted_iota(i32, shape, dim)


def taper(offset):
    distance = jnp.abs(offset)
    spread = distance.astype(f32)
    value = (1.0 - spread / (REACH + 1)) * jnp.exp(-spread / 3.0)
    return jnp.where(distance <= REACH, value, 0.0)


def split(x):
    high = x.astype(bf16)
    return high, (x - high.astype(f32)).astype(bf16)


def both(x):
    return jnp.concatenate(split(x), axis=1)


def three(x):
    high = x.astype(bf16)
    rest = x - high.astype(f32)
    middle = rest.astype(bf16)
    return jnp.concatenate([high, middle, (rest - middle.astype(f32)).astype(bf16)], axis=0)


def dot(a, b):
    return lax.dot_general(a, b, (((1,), (0,)), ((), ())), preferred_element_type=f32)


def dot_nt(a, b):
    return lax.dot_general(a, b, (((1,), (1,)), ((), ())), preferred_element_type=f32)


def quad(ref, weight):
    high, rest = split(weight)
    ref[0:CY, :] = jnp.concatenate([high, rest], axis=1)
    ref[CY : 2 * CY, :] = jnp.concatenate([high, jnp.zeros_like(high)], axis=1)


def halves(x):
    return x[:, :CY] + x[:, CY:]


def fold(x):
    rows, cols = x.shape
    total = jnp.zeros((8, CY), f32)
    for c in range(cols // CY):
        total = total + jnp.sum(x[:, c * CY : (c + 1) * CY].reshape(rows // 8, 8, CY), axis=0)
    return total


def lane_step(lane, side):
    pair = lane >> 7
    place = (lane >> 3) & 15
    slot, odd = place >> 1, place & 1
    if side == 0:
        return 16 * pair + 8 * odd + slot
    return 16 * pair + jnp.where(odd == 1, slot, 8 + ((slot + 7) & 7))


def kernel(
    n_row,
    n_col,
    grid_hbm,
    noise_ref,
    obs_hbm,
    site_noise_ref,
    offset_hbm,
    cell_ref,
    count_ref,
    cov_ref,
    first,
    second,
    start_out,
    site_out,
    coef_out,
    grid,
    merged,
    mixed,
    smooth,
    obs_ref,
    offset_ref,
    slots,
    pack,
    row_halo,
    col_halo,
    row_sums,
    col_sums,
    cov_time,
    cov_side,
    band_row,
    band_col,
    halo_rows,
    spread,
    gather,
    order,
    site_row,
    site_along,
    site_value,
    site_first,
    site_image,
    site_extra,
    list_vmem,
    lists,
    local_sem,
    list_sem,
    send_sem,
    recv_sem,
    row_send,
    row_recv,
    col_send,
    col_recv,
):
    me_row = lax.axis_index("row")
    me_col = lax.axis_index("col")

    loads = [
        pltpu.make_async_copy(obs_hbm.at[step, 0], obs_ref.at[step : step + 1], local_sem.at[step])
        for step in range(STEPS)
    ]
    for part in range(2):
        loads.append(
            pltpu.make_async_copy(
                offset_hbm.at[part, 0],
                offset_ref.at[part : part + 1],
                local_sem.at[STEPS + part],
            )
        )
    for copy in loads:
        copy.start()
    load = pltpu.make_async_copy(grid_hbm, grid, local_sem.at[STEPS + 2])
    load.start()

    barrier = pltpu.get_barrier_semaphore()
    for step in range(1, n_row):
        pl.semaphore_signal(
            barrier, inc=1, device_id=(lax.rem(me_row + step, n_row), me_col), device_id_type=MESH
        )
    for step in range(1, n_col):
        pl.semaphore_signal(
            barrier, inc=1, device_id=(me_row, lax.rem(me_col + step, n_col)), device_id_type=MESH
        )

    def exists(down, right):
        row, col = me_row + down, me_col + right
        return (row >= 0) & (row < n_row) & (col >= 0) & (col < n_col)

    diagonals = [(-1, -1), (-1, 1), (1, -1), (1, 1)]
    for down, right in diagonals:

        @pl.when(exists(down, right))
        def _():
            pl.semaphore_signal(
                barrier, inc=1, device_id=(me_row + down, me_col + right), device_id_type=MESH
            )

    @pl.when(me_row == 0)
    def _():
        row_halo[:, 0] = jnp.zeros((2, STEPS, 8, CY), f32)
        col_halo[:, :, :, 0:8, :] = jnp.zeros((2, 2, 2, 8, CY), f32)

    @pl.when(me_row == n_row - 1)
    def _():
        row_halo[:, 1] = jnp.zeros((2, STEPS, 8, CY), f32)
        col_halo[:, :, :, HIGH - 8 : HIGH, :] = jnp.zeros((2, 2, 2, 8, CY), f32)

    @pl.when(me_col == 0)
    def _():
        col_halo[:, 0] = jnp.zeros((2, 2, HIGH, CY), f32)

    @pl.when(me_col == n_col - 1)
    def _():
        col_halo[:, 1] = jnp.zeros((2, 2, HIGH, CY), f32)

    slots[ZERO] = jnp.zeros((CX, CY), f32)

    cell = cell_ref[...]
    row_of = cell >> 7
    key = row_of * SLOT + iota((1, SLOT), 1)
    counts = [jnp.zeros((1, CHUNK), i32) for _ in range(CHUNKS)]
    for j in range(CHUNKS):
        own = jnp.broadcast_to(key[:, j * CHUNK : (j + 1) * CHUNK], (CHUNK, CHUNK)).T
        for k in range(CHUNKS):
            less = own < key[:, k * CHUNK : (k + 1) * CHUNK]
            counts[k] = counts[k] + jnp.sum(jnp.where(less, 1, 0), axis=0, keepdims=True)
    rank = jnp.concatenate(counts, axis=1)
    for j in range(CHUNKS):
        place = iota((CHUNK, SLOT), 0) + j * CHUNK
        order[j * CHUNK : (j + 1) * CHUNK, :] = jnp.where(place == rank, 1.0, 0.0).astype(bf16)

    lead = iota((CHUNKS, SLOT), 0) * CHUNK
    ranks = jnp.broadcast_to(rank, (CHUNKS, SLOT))
    rows_of = jnp.broadcast_to(row_of, (CHUNKS, SLOT))
    lowest = jnp.min(jnp.where(ranks >= lead, rows_of, CX), axis=1, keepdims=True) >> 3
    highest = (jnp.max(jnp.where(ranks < lead + CHUNK, rows_of, 0), axis=1, keepdims=True) + 1) >> 3
    low = [lowest[j : j + 1, :] for j in range(CHUNKS)]
    top = [highest[j : j + 1, :] for j in range(CHUNKS)]
    begin = [jnp.zeros((1, 1), i32)]
    for j in range(CHUNKS):
        begin.append(begin[j] + top[j] - low[j] + 1)
    lane = iota((1, CHUNK), 1)
    one, none = jnp.ones((1, CHUNK), i32), jnp.zeros((1, CHUNK), i32)
    chunk_of = none
    for j in range(1, CHUNKS):
        chunk_of = chunk_of + jnp.where(begin[j] <= lane, one, none)

    def choose(which, values):
        result = jnp.broadcast_to(values[0], (1, CHUNK))
        for j in range(1, CHUNKS):
            result = jnp.where(which == j, values[j], result)
        return result

    start_of = choose(chunk_of, begin)
    group_of = jnp.minimum(choose(chunk_of, low) + lane - start_of, GROUPS - 1)
    blank = jnp.full((1, 1), -1, i32)
    link = choose(chunk_of, [blank] + begin[: CHUNKS - 1]) + group_of
    link = link - choose(chunk_of, [blank] + low[:-1])
    link = jnp.where(group_of <= choose(chunk_of, [blank] + top[:-1]), link, ZERO)
    last = none - 1
    for j in range(CHUNKS):
        last = last + jnp.where(low[j] <= lane, one, none)
    final = choose(last, begin) + lane - choose(last, low)
    final = jnp.where((last >= 0) & (choose(last, top) >= lane), final, ZERO)
    ends = none
    for j in range(CHUNKS):
        ends = jnp.where(lane == j, begin[j + 1] - 1, ends)
    listed = [chunk_of, group_of, link, jnp.where(lane == start_of, ZERO, lane - 1), final, ends]
    for row, values in enumerate(listed):
        list_vmem[row : row + 1, :] = jnp.clip(values, 0, ZERO)
    list_vmem[6:8, :] = jnp.zeros((2, CHUNK), i32)
    listing = pltpu.make_async_copy(list_vmem, lists, list_sem)
    listing.start()

    for copy in loads:
        copy.wait()
    live = jnp.where(iota((1, SLOT), 1) < count_ref[...], 1.0, 0.0)
    start_out[...] = live * obs_ref[...]
    carried = jnp.concatenate(
        [
            start_out[...],
            offset_ref[...],
            site_noise_ref[...],
            live,
            row_of.astype(f32),
            (cell & (CY - 1)).astype(f32),
            jnp.zeros((10, SLOT), f32),
        ],
        axis=0,
    )
    placed = dot_nt(three(carried), order[...])
    placed = placed[0:48] + placed[48:96] + placed[96:144]
    site_first[...] = placed[0:STEPS]
    site_extra[...] = placed[STEPS : STEPS + 8]

    def column_weight(j):
        here = slice(j * CHUNK, (j + 1) * CHUNK)
        along, col = site_extra[1:2, here], site_extra[5:6, here].astype(i32)
        column = iota((CY, CHUNK), 0)
        weight = jnp.where(column == col, 1.0 - along, 0.0)
        return weight + jnp.where(column == col + 1, along, 0.0)

    for j in range(CHUNKS):
        here = slice(j * CHUNK, (j + 1) * CHUNK)
        site_row[j] = jnp.broadcast_to(placed[36:37, here].astype(i32), (8, CHUNK))
        site_along[j] = jnp.broadcast_to(placed[32:33, here], (8, CHUNK))
        quad(spread.at[j], column_weight(j).T)

    listing.wait()
    load.wait()

    signals = (n_row - 1) + (n_col - 1)
    for down, right in diagonals:
        signals = signals + jnp.where(exists(down, right), 1, 0)
    pl.semaphore_wait(barrier, signals)

    def prepare_filters():
        for j in range(CHUNKS):
            quad(gather.at[j], column_weight(j))
        cov_high, cov_rest = split(cov_ref[...])
        eights = [
            lambda x: x >> 3,
            functools.partial(lane_step, side=0),
            functools.partial(lane_step, side=1),
        ]
        same = (iota((2 * CY, 2 * CY), 0) & 7) == (iota((2 * CY, 2 * CY), 1) & 7)
        for kind, step_of in enumerate(eights):
            tall = jnp.where(step_of(iota((2 * CY, STEPS), 0)) == iota((2 * CY, STEPS), 1), 1.0, 0.0)
            wide = jnp.where(step_of(iota((STEPS, 2 * CY), 1)) == iota((STEPS, 2 * CY), 0), 1.0, 0.0)
            tall, wide = tall.astype(bf16), wide.astype(bf16)
            for part, values in enumerate((cov_high, cov_rest)):
                block = dot(tall, dot(values, wide).astype(bf16))
                block = jnp.where(same, block, 0.0).astype(bf16)
                if kind == 0:
                    cov_time[part] = block
                else:
                    cov_side[kind - 1, part] = block
        high, rest = split(taper(iota((CHUNK, CHUNK + 16), 1) - 8 - iota((CHUNK, CHUNK + 16), 0)))
        band_row[0:CHUNK] = high
        band_row[CHUNK : 2 * CHUNK] = rest

        line, column = iota((CY, CY), 0), iota((CY, CY), 1)
        own = taper(line - column)
        from_left = taper(column + 8 - (line & 7))
        from_right = taper(CY + (line & 7) - column)

        def fill_halo(index, _):
            left = 2 * (index & 7) + (index >> 3)
            right = (left + 1) & 15
            place = line >> 3
            weight = jnp.where(place == left, from_left, 0.0)
            weight = weight + jnp.where(place == right, from_right, 0.0)
            quad(band_col.at[index, 0 : 2 * CY], own)
            quad(band_col.at[index, 2 * CY : 4 * CY], weight)
            return 0

        lax.fori_loop(0, 16, fill_halo, 0)


    def row_weight(chunk, group):
        row = site_row[chunk] - 8 * group
        along = site_along[chunk]
        line = iota((8, CHUNK), 0)
        return jnp.where(row == line, 1.0 - along, 0.0) + jnp.where(row + 1 == line, along, 0.0)

    def messages(call, part):
        field, rows = merged.at[call], slice(part * PART, (part + 1) * PART)
        there = slice(8 + part * PART, 8 + (part + 1) * PART)
        table = []
        if part == 0:
            table += [
                (-1, 0, field.at[:, 0:8, :], row_halo.at[call, 1]),
                (-1, 1, pack.at[0, :, 0:8, :], col_halo.at[call, 0, :, HIGH - 8 : HIGH, :]),
                (-1, -1, pack.at[1, :, 0:8, :], col_halo.at[call, 1, :, HIGH - 8 : HIGH, :]),
            ]
        if part == PARTS - 1:
            table += [
                (1, 0, field.at[:, CX - 8 : CX, :], row_halo.at[call, 0]),
                (1, 1, pack.at[0, :, CX - 8 : CX, :], col_halo.at[call, 0, :, 0:8, :]),
                (1, -1, pack.at[1, :, CX - 8 : CX, :], col_halo.at[call, 1, :, 0:8, :]),
            ]
        table += [
            (0, 1, pack.at[0, :, rows, :], col_halo.at[call, 0, :, there, :]),
            (0, -1, pack.at[1, :, rows, :], col_halo.at[call, 1, :, there, :]),
        ]
        return [
            (
                down,
                right,
                pltpu.make_async_remote_copy(
                    src_ref=source,
                    dst_ref=target,
                    send_sem=send_sem.at[call, part, index],
                    recv_sem=recv_sem.at[call, part, index],
                    device_id=(me_row + down, me_col + right),
                    device_id_type=MESH,
                ),
            )
            for index, (down, right, source, target) in enumerate(table)
        ]

    def mix(values):
        rhs = both(values)
        return halves(dot(cov_time[0], rhs)) + dot(cov_time[1], rhs[:, :CY])

    def sweep_rows(values):
        result = dot(band_row[...], both(values))
        return halves(result[0:CHUNK]) + result[CHUNK : 2 * CHUNK, 0:CY]

    def sum_start(call, parts):
        lane = iota((1, CY), 1)
        line = jnp.zeros((1, CY), f32)
        for index, part in enumerate(parts):
            part = jnp.sum(jnp.sum(part, axis=0, keepdims=True), axis=1, keepdims=True)
            line = jnp.where(lane == index, part, line)
        row_sums[call, pl.ds(me_row, 1), 0:1, :] = line[None]
        copies = []
        for step in range(1, n_row):
            copy = pltpu.make_async_remote_copy(
                src_ref=row_sums.at[call, me_row, 0:1],
                dst_ref=row_sums.at[call, me_row, 0:1],
                send_sem=row_send.at[call, step],
                recv_sem=row_recv.at[call, step],
                device_id=(lax.rem(me_row + step, n_row), me_col),
                device_id_type=MESH,
            )
            copy.start()
            copies.append(copy)
        return copies

    def sum_cross(call, copies):
        for copy in copies:
            copy.wait()
        line = row_sums[call, 0, 0:1]
        for index in range(1, n_row):
            line = line + row_sums[call, index, 0:1]
        col_sums[call, pl.ds(me_col, 1), 0:1, :] = line[None]
        copies = []
        for step in range(1, n_col):
            copy = pltpu.make_async_remote_copy(
                src_ref=col_sums.at[call, me_col, 0:1],
                dst_ref=col_sums.at[call, me_col, 0:1],
                send_sem=col_send.at[call, step],
                recv_sem=col_recv.at[call, step],
                device_id=(me_row, lax.rem(me_col + step, n_col)),
                device_id_type=MESH,
            )
            copy.start()
            copies.append(copy)
        return copies

    def sum_end(call, copies):
        for copy in copies:
            copy.wait()
        line = col_sums[call, 0, 0:1]
        for index in range(1, n_col):
            line = line + col_sums[call, index, 0:1]
        return [line[:, index : index + 1] for index in range(3)]

    def spread_sites(sites):
        values = sites * site_live
        for j in range(CHUNKS):
            part = values[:, j * CHUNK : (j + 1) * CHUNK]
            site_value[j] = jnp.broadcast_to(part[:, None, :], (STEPS, 8, CHUNK))

        def scatter(pair, _):
            chunk, group, link = lists[0, pair], lists[1, pair], lists[2, pair]
            value = site_value[chunk] * row_weight(chunk, group)[None]
            result = dot(both(value.reshape(CX, CHUNK)), spread[chunk])
            slots[pair] = halves(result) + slots[link]
            return 0

        lax.fori_loop(0, PAIRS, scatter, 0, unroll=16)

    def exchange(call, source):
        def join(group, _):
            here = pl.ds(pl.multiple_of(8 * group, 8), 8)
            values = source[:, here, :] + slots[lists[4, group]].reshape(STEPS, 8, CY)
            merged[call, :, here, :] = values
            place = iota((8, CY), 1) >> 3
            for pair in range(2):
                ahead = jnp.zeros((8, CY), f32)
                behind = jnp.zeros((8, CY), f32)
                for step in range(16):
                    slot = 2 * (step & 7) + (step >> 3)
                    beside = (slot + 1) & 15
                    rolled = values[16 * pair + step]
                    if beside:
                        rolled = pltpu.roll(rolled, 8 * beside, 1)
                    ahead = jnp.where(place == slot, rolled, ahead)
                    behind = jnp.where(place == beside, rolled, behind)
                pack[0, pair, here, :] = ahead
                pack[1, pair, here, :] = behind
            return 0

        width = GROUPS // PARTS
        halo = []
        for part in (0, PARTS - 1, *range(1, PARTS - 1)):
            lax.fori_loop(part * width, (part + 1) * width, join, 0, unroll=8)
            ready = messages(call, part)
            for down, right, copy in ready:

                @pl.when(exists(down, right))
                def _():
                    copy.start()

            halo += ready
        return halo

    def mix_steps(call):
        def temporal(group, _):
            here = pl.ds(pl.multiple_of(8 * group, 8), 8)
            values = mix(merged[call, :, here, :].reshape(CX, CY))
            there = pl.ds(pl.multiple_of(8 * group + 8, 8), 8)
            mixed[0:STEPS, there, :] = values.reshape(STEPS, 8, CY)
            return 0

        lax.fori_loop(0, GROUPS, temporal, 0, unroll=16)

    def take_halo(call, halo):
        for down, right, copy in halo:

            @pl.when(exists(down, right))
            def _():
                copy.wait_send()

            @pl.when(exists(-down, -right))
            def _():
                copy.wait_recv()

        for side, first_row in ((0, 0), (1, HIGH - 8)):
            values = mix(row_halo[call, side].reshape(CX, CY))
            mixed[0:STEPS, first_row : first_row + 8, :] = values.reshape(STEPS, 8, CY)
        sides = []
        for side in range(2):
            values = jnp.concatenate([col_halo[call, side, 0], col_halo[call, side, 1]], axis=1)
            high, rest = split(values)
            weight = cov_side[side, 0]
            sides.append(dot(high, weight) + dot(rest, weight) + dot(high, cov_side[side, 1]))
        even = ((iota((HIGH, CY), 1) >> 3) & 1) == 0
        for pair in range(2):
            left = sides[0][:, pair * CY : (pair + 1) * CY]
            right = sides[1][:, pair * CY : (pair + 1) * CY]
            mixed[STEPS + 2 * pair] = jnp.where(even, left, right)
            mixed[STEPS + 2 * pair + 1] = jnp.where(even, right, left)
        for index in range(4):
            for block in range(2):
                rows = slice(block * CHUNK, (block + 1) * CHUNK)
                window = slice(block * CHUNK, block * CHUNK + CHUNK + 16)
                halo_rows[index, rows, :] = both(sweep_rows(mixed[STEPS + index, window, :]))

    def filtered(step):
        swept = [
            both(sweep_rows(mixed[step, block * CHUNK : block * CHUNK + CHUNK + 16, :]))
            for block in range(2)
        ]
        swept = jnp.concatenate([jnp.concatenate(swept, axis=0), halo_rows[step >> 3]], axis=1)
        return 0.25 * halves(dot(swept, band_col[step & 15]))

    def totals(body, count):
        start = (jnp.zeros((8, CY), f32),) * count

        def sweep(step, sums):
            return tuple(total + fold(term) for total, term in zip(sums, body(step)))

        return lax.fori_loop(0, STEPS, sweep, start, unroll=16)

    def first_sweep(step):
        field, own = filtered(step), grid[step]
        weighted = noise_ref[...] * own
        smooth[:, step] = field.reshape(GROUPS, 8, CY)
        first[step] = field + weighted
        return own * own, merged[0, step] * field + weighted * own

    def collect_sites(sites):
        def collect(pair, _):
            chunk, group, link = lists[0, pair], lists[1, pair], lists[3, pair]
            values = both(smooth[group].reshape(CX, CY))
            result = halves(dot(values, gather[chunk])).reshape(STEPS, 8, CHUNK)
            result = result * row_weight(chunk, group)[None]
            slots[pair] = result.reshape(CX, CHUNK) + slots[link]
            return 0

        lax.fori_loop(0, PAIRS, collect, 0, unroll=16)
        for j in range(CHUNKS):
            here = slice(j * CHUNK, (j + 1) * CHUNK)
            total = jnp.sum(slots[lists[5, j]].reshape(STEPS, 8, CHUNK), axis=1)
            site_image[:, here] = site_live[:, here] * total + site_weight[:, here] * sites[:, here]

    site_live = site_extra[3:4, :]
    site_weight = site_live * site_extra[2:3, :] + (1.0 - site_live)
    start = site_first[...]

    spread_sites(start)
    halo = exchange(0, grid)
    prepare_filters()
    mix_steps(0)
    take_halo(0, halo)
    sums = totals(first_sweep, 2)
    square = start * start
    terms = square, site_weight * square
    pending = sum_start(0, [total + fold(term) for total, term in zip(sums, terms)])
    collect_sites(start)

    once = site_image[...]
    spread_sites(once)
    pending = sum_cross(0, pending)
    halo = exchange(1, first)
    restored = dot(three(once), order[...])
    site_out[...] = restored[0:STEPS] + restored[STEPS : 2 * STEPS] + restored[2 * STEPS :]
    mix_steps(1)
    norm, across, _ = sum_end(0, pending)
    alpha = norm / across
    take_halo(1, halo)

    def second_sweep(step):
        field, own, image = filtered(step), grid[step], first[step]
        second[step] = field + noise_ref[...] * image
        residual = own - alpha * image
        joined = merged[0, step] - alpha * merged[1, step]
        through = smooth[:, step].reshape(CX, CY) - alpha * field
        square = residual * residual
        return square, joined * through + noise_ref[...] * square, residual * image

    sums = totals(second_sweep, 3)
    residual = start - alpha * once
    square = residual * residual
    terms = square, site_weight * square, residual * once
    pending = sum_start(1, [total + fold(term) for total, term in zip(sums, terms)])
    after, applied, cross = sum_end(1, sum_cross(1, pending))
    beta = after / norm
    alpha_next = after / (applied + beta * (2.0 * cross + beta * across))
    line = iota((8, CY), 0)
    direct = alpha + alpha_next * (1.0 + beta)
    coef_out[...] = jnp.where(line == 0, direct, -(alpha * alpha_next))


def close_kernel(
    coef_ref, first, second, start, image, grid_ref, solution_ref, residual_ref, sites_hbm, sites, sems
):
    index = pl.program_id(0)
    direct, cross = coef_ref[0:1, 0:1], coef_ref[1:2, 0:1]
    copies = [
        pltpu.make_async_copy(sites.at[step : step + 1], sites_hbm.at[step, 0], sems.at[step])
        for step in range(STEPS)
    ]

    @pl.when(index == 0)
    def _():
        sites[...] = direct * start[...] + cross * image[...]
        for copy in copies:
            copy.start()

    count = grid_ref.shape[0]
    for step in range(count):
        own = grid_ref[step]
        once = first[index * count + step]
        twice = second[index * count + step]
        solution_ref[step] = direct * own + cross * once
        residual_ref[step] = own - direct * once - cross * twice

    @pl.when(index == pl.num_programs(0) - 1)
    def _():
        for copy in copies:
            copy.wait()


def body(
    n_row,
    n_col,
    grid_obs,
    grid_noise,
    station_obs,
    station_noise,
    station_offset,
    station_cell,
    station_count,
    time_cov,
):
    vmem = pl.BlockSpec(memory_space=pltpu.VMEM)
    anywhere = pl.BlockSpec(memory_space=pl.ANY)
    field = (STEPS, CX, CY)
    dma = pltpu.SemaphoreType.DMA
    first, second, start, image, coef = pl.pallas_call(
        functools.partial(kernel, n_row, n_col),
        out_shape=(
            pltpu.VMEM(field, f32),
            pltpu.VMEM(field, f32),
            pltpu.VMEM((STEPS, SLOT), f32),
            pltpu.VMEM((STEPS, SLOT), f32),
            pltpu.VMEM((8, CY), f32),
        ),
        in_specs=[anywhere, vmem, anywhere, vmem, anywhere, vmem, vmem, vmem],
        out_specs=(vmem,) * 5,
        scratch_shapes=[
            pltpu.VMEM(field, f32),
            pltpu.VMEM((2, STEPS, CX, CY), f32),
            pltpu.VMEM((STEPS + 4, HIGH, CY), f32),
            pltpu.VMEM((GROUPS, STEPS, 8, CY), f32),
            pltpu.VMEM((STEPS, SLOT), f32),
            pltpu.VMEM((2, SLOT), f32),
            pltpu.VMEM((ZERO + 1, CX, CY), f32),
            pltpu.VMEM((2, 2, CX, CY), f32),
            pltpu.VMEM((2, 2, STEPS, 8, CY), f32),
            pltpu.VMEM((2, 2, 2, HIGH, CY), f32),
            pltpu.VMEM((2, n_row, 8, CY), f32),
            pltpu.VMEM((2, n_col, 8, CY), f32),
            pltpu.VMEM((2, 2 * CY, 2 * CY), bf16),
            pltpu.VMEM((2, 2, 2 * CY, 2 * CY), bf16),
            pltpu.VMEM((2 * CHUNK, CHUNK + 16), bf16),
            pltpu.VMEM((16, 4 * CY, 2 * CY), bf16),
            pltpu.VMEM((4, CX, 2 * CY), bf16),
            pltpu.VMEM((CHUNKS, 2 * CY, 2 * CHUNK), bf16),
            pltpu.VMEM((CHUNKS, 2 * CY, 2 * CHUNK), bf16),
            pltpu.VMEM((SLOT, SLOT), bf16),
            pltpu.VMEM((CHUNKS, 8, CHUNK), i32),
            pltpu.VMEM((CHUNKS, 8, CHUNK), f32),
            pltpu.VMEM((CHUNKS, STEPS, 8, CHUNK), f32),
            pltpu.VMEM((STEPS, SLOT), f32),
            pltpu.VMEM((STEPS, SLOT), f32),
            pltpu.VMEM((8, SLOT), f32),
            pltpu.VMEM((8, CHUNK), i32),
            pltpu.SMEM((8, CHUNK), i32),
            dma((STEPS + 3,)),
            dma,
            dma((2, PARTS, 5)),
            dma((2, PARTS, 5)),
            dma((2, n_row)),
            dma((2, n_row)),
            dma((2, n_col)),
            dma((2, n_col)),
        ],
        compiler_params=pltpu.CompilerParams(
            collective_id=0, has_side_effects=True, vmem_limit_bytes=48 * 2**20
        ),
        name="kriging",
    )(
        grid_obs,
        grid_noise,
        station_obs,
        station_noise.reshape(1, SLOT),
        station_offset,
        station_cell.reshape(1, SLOT),
        station_count,
        time_cov,
    )
    block = pl.BlockSpec((CLOSE, CX, CY), lambda index: (index, 0, 0))
    solution_grid, residual_grid, solution_sites = pl.pallas_call(
        close_kernel,
        grid=(STEPS // CLOSE,),
        out_shape=(
            jax.ShapeDtypeStruct(field, f32),
            jax.ShapeDtypeStruct(field, f32),
            jax.ShapeDtypeStruct((STEPS, 1, 1, SLOT), f32),
        ),
        in_specs=[vmem] * 5 + [block],
        out_specs=(block, block, anywhere),
        scratch_shapes=[pltpu.VMEM((STEPS, SLOT), f32), dma((STEPS,))],
        compiler_params=pltpu.CompilerParams(vmem_limit_bytes=16 * 2**20),
        name="close",
    )(coef, first, second, start, image, grid_obs)
    return solution_grid, solution_sites, residual_grid


def solution(mesh):
    placed = (
        P(None, "row", "col"),
        P("row", "col"),
        P(None, "row", "col", None),
        P("row", "col", None),
        P(None, "row", "col", None),
        P("row", "col", None),
        P("row", "col"),
        P(),
    )
    return jax.shard_map(
        functools.partial(body, mesh.shape["row"], mesh.shape["col"]),
        mesh=mesh,
        in_specs=placed,
        out_specs=(P(None, "row", "col"), P(None, "row", "col", None), P(None, "row", "col")),
        check_vma=False,
    )
```

```python
import functools

import jax
import jax.numpy as jnp
from jax import lax
from jax.experimental import pallas as pl
from jax.experimental.pallas import tpu as pltpu
from jax.sharding import PartitionSpec as P

REACH = 8
CLOSE = 2
CX = 256
CY = 128
STEPS = 32
SLOT = 1024
CHUNK = 128
CHUNKS = SLOT // CHUNK
GROUPS = CX // 8
PARTS = 4
PART = CX // PARTS
PAIRS = GROUPS + 2 * CHUNKS - 2
ZERO = PAIRS
HIGH = CX + 2 * REACH
MESH = pl.DeviceIdType.MESH
f32, bf16, i32 = jnp.float32, jnp.bfloat16, jnp.int32


def iota(shape, dim):
    return lax.broadcasted_iota(i32, shape, dim)


def taper(offset):
    distance = jnp.abs(offset)
    spread = distance.astype(f32)
    value = (1.0 - spread / (REACH + 1)) * jnp.exp(-spread / 3.0)
    return jnp.where(distance <= REACH, value, 0.0)


def split(x):
    high = x.astype(bf16)
    return high, (x - high.astype(f32)).astype(bf16)


def both(x):
    return jnp.concatenate(split(x), axis=1)


def three(x):
    high = x.astype(bf16)
    rest = x - high.astype(f32)
    middle = rest.astype(bf16)
    return jnp.concatenate([high, middle, (rest - middle.astype(f32)).astype(bf16)], axis=0)


def dot(a, b):
    return lax.dot_general(a, b, (((1,), (0,)), ((), ())), preferred_element_type=f32)


def dot_nt(a, b):
    return lax.dot_general(a, b, (((1,), (1,)), ((), ())), preferred_element_type=f32)


def quad(ref, weight):
    high, rest = split(weight)
    ref[0:CY, :] = jnp.concatenate([high, rest], axis=1)
    ref[CY : 2 * CY, :] = jnp.concatenate([high, jnp.zeros_like(high)], axis=1)


def halves(x):
    return x[:, :CY] + x[:, CY:]


def fold(x):
    rows, cols = x.shape
    total = jnp.zeros((8, CY), f32)
    for c in range(cols // CY):
        total = total + jnp.sum(x[:, c * CY : (c + 1) * CY].reshape(rows // 8, 8, CY), axis=0)
    return total


def lane_step(lane, side):
    pair = lane >> 7
    place = (lane >> 3) & 15
    slot, odd = place >> 1, place & 1
    if side == 0:
        return 16 * pair + 8 * odd + slot
    return 16 * pair + jnp.where(odd == 1, slot, 8 + ((slot + 7) & 7))


def kernel(
    n_row,
    n_col,
    grid_hbm,
    noise_ref,
    obs_hbm,
    site_noise_ref,
    offset_hbm,
    cell_ref,
    count_ref,
    cov_ref,
    first,
    second,
    start_out,
    site_out,
    coef_out,
    grid,
    merged,
    mixed,
    smooth,
    obs_ref,
    offset_ref,
    slots,
    pack,
    row_halo,
    col_halo,
    row_sums,
    col_sums,
    cov_time,
    cov_side,
    wide_band,
    band_row,
    band_own,
    band_edge,
    edges,
    spread,
    gather,
    order,
    site_row,
    site_along,
    site_value,
    site_first,
    site_image,
    site_extra,
    list_vmem,
    lists,
    local_sem,
    list_sem,
    send_sem,
    recv_sem,
    row_send,
    row_recv,
    col_send,
    col_recv,
):
    me_row = lax.axis_index("row")
    me_col = lax.axis_index("col")

    loads = [
        pltpu.make_async_copy(obs_hbm.at[:, 0], obs_ref, local_sem.at[0]),
        pltpu.make_async_copy(offset_hbm.at[:, 0], offset_ref, local_sem.at[1]),
    ]
    for copy in loads:
        copy.start()
    load = pltpu.make_async_copy(grid_hbm, grid, local_sem.at[2])
    load.start()

    barrier = pltpu.get_barrier_semaphore()
    for step in range(1, n_row):
        pl.semaphore_signal(
            barrier, inc=1, device_id=(lax.rem(me_row + step, n_row), me_col), device_id_type=MESH
        )
    for step in range(1, n_col):
        pl.semaphore_signal(
            barrier, inc=1, device_id=(me_row, lax.rem(me_col + step, n_col)), device_id_type=MESH
        )

    def exists(down, right):
        row, col = me_row + down, me_col + right
        return (row >= 0) & (row < n_row) & (col >= 0) & (col < n_col)

    diagonals = [(-1, -1), (-1, 1), (1, -1), (1, 1)]
    for down, right in diagonals:

        @pl.when(exists(down, right))
        def _():
            pl.semaphore_signal(
                barrier, inc=1, device_id=(me_row + down, me_col + right), device_id_type=MESH
            )

    @pl.when(me_row == 0)
    def _():
        row_halo[:, 0] = jnp.zeros((2, STEPS, 8, CY), f32)
        col_halo[:, :, :, 0:8, :] = jnp.zeros((2, 2, 2, 8, CY), f32)

    @pl.when(me_row == n_row - 1)
    def _():
        row_halo[:, 1] = jnp.zeros((2, STEPS, 8, CY), f32)
        col_halo[:, :, :, HIGH - 8 : HIGH, :] = jnp.zeros((2, 2, 2, 8, CY), f32)

    @pl.when(me_col == 0)
    def _():
        col_halo[:, 0] = jnp.zeros((2, 2, HIGH, CY), f32)

    @pl.when(me_col == n_col - 1)
    def _():
        col_halo[:, 1] = jnp.zeros((2, 2, HIGH, CY), f32)

    slots[ZERO] = jnp.zeros((CX, CY), f32)

    cell = cell_ref[...]
    row_of = cell >> 7
    key = row_of * SLOT + iota((1, SLOT), 1)
    counts = [jnp.zeros((1, CHUNK), i32) for _ in range(CHUNKS)]
    for j in range(CHUNKS):
        own = jnp.broadcast_to(key[:, j * CHUNK : (j + 1) * CHUNK], (CHUNK, CHUNK)).T
        for k in range(CHUNKS):
            less = own < key[:, k * CHUNK : (k + 1) * CHUNK]
            counts[k] = counts[k] + jnp.sum(jnp.where(less, 1, 0), axis=0, keepdims=True)
    rank = jnp.concatenate(counts, axis=1)
    for j in range(CHUNKS):
        place = iota((CHUNK, SLOT), 0) + j * CHUNK
        order[j * CHUNK : (j + 1) * CHUNK, :] = jnp.where(place == rank, 1.0, 0.0).astype(bf16)

    lead = iota((CHUNKS, SLOT), 0) * CHUNK
    ranks = jnp.broadcast_to(rank, (CHUNKS, SLOT))
    rows_of = jnp.broadcast_to(row_of, (CHUNKS, SLOT))
    lowest = jnp.min(jnp.where(ranks >= lead, rows_of, CX), axis=1, keepdims=True) >> 3
    highest = (jnp.max(jnp.where(ranks < lead + CHUNK, rows_of, 0), axis=1, keepdims=True) + 1) >> 3
    low = [lowest[j : j + 1, :] for j in range(CHUNKS)]
    top = [highest[j : j + 1, :] for j in range(CHUNKS)]
    begin = [jnp.zeros((1, 1), i32)]
    for j in range(CHUNKS):
        begin.append(begin[j] + top[j] - low[j] + 1)
    lane = iota((1, CHUNK), 1)
    one, none = jnp.ones((1, CHUNK), i32), jnp.zeros((1, CHUNK), i32)
    chunk_of = none
    for j in range(1, CHUNKS):
        chunk_of = chunk_of + jnp.where(begin[j] <= lane, one, none)

    def choose(which, values):
        result = jnp.broadcast_to(values[0], (1, CHUNK))
        for j in range(1, CHUNKS):
            result = jnp.where(which == j, values[j], result)
        return result

    start_of = choose(chunk_of, begin)
    group_of = jnp.minimum(choose(chunk_of, low) + lane - start_of, GROUPS - 1)
    blank = jnp.full((1, 1), -1, i32)
    link = choose(chunk_of, [blank] + begin[: CHUNKS - 1]) + group_of
    link = link - choose(chunk_of, [blank] + low[:-1])
    link = jnp.where(group_of <= choose(chunk_of, [blank] + top[:-1]), link, ZERO)
    last = none - 1
    for j in range(CHUNKS):
        last = last + jnp.where(low[j] <= lane, one, none)
    final = choose(last, begin) + lane - choose(last, low)
    final = jnp.where((last >= 0) & (choose(last, top) >= lane), final, ZERO)
    ends = none
    for j in range(CHUNKS):
        ends = jnp.where(lane == j, begin[j + 1] - 1, ends)
    listed = [chunk_of, group_of, link, jnp.where(lane == start_of, ZERO, lane - 1), final, ends]
    for row, values in enumerate(listed):
        list_vmem[row : row + 1, :] = jnp.clip(values, 0, ZERO)
    list_vmem[6:8, :] = jnp.zeros((2, CHUNK), i32)
    listing = pltpu.make_async_copy(list_vmem, lists, list_sem)
    listing.start()

    for copy in loads:
        copy.wait()
    live = jnp.where(iota((1, SLOT), 1) < count_ref[...], 1.0, 0.0)
    start_out[...] = live * obs_ref[...].reshape(STEPS, SLOT)
    carried = jnp.concatenate(
        [
            start_out[...],
            offset_ref[...].reshape(2, SLOT),
            site_noise_ref[...],
            live,
            row_of.astype(f32),
            (cell & (CY - 1)).astype(f32),
            jnp.zeros((10, SLOT), f32),
        ],
        axis=0,
    )
    placed = dot_nt(three(carried), order[...])
    placed = placed[0:48] + placed[48:96] + placed[96:144]
    site_first[...] = placed[0:STEPS]
    site_extra[...] = placed[STEPS : STEPS + 8]

    def column_weight(j):
        here = slice(j * CHUNK, (j + 1) * CHUNK)
        along, col = site_extra[1:2, here], site_extra[5:6, here].astype(i32)
        column = iota((CY, CHUNK), 0)
        weight = jnp.where(column == col, 1.0 - along, 0.0)
        return weight + jnp.where(column == col + 1, along, 0.0)

    for j in range(CHUNKS):
        here = slice(j * CHUNK, (j + 1) * CHUNK)
        site_row[j] = jnp.broadcast_to(placed[36:37, here].astype(i32), (8, CHUNK))
        site_along[j] = jnp.broadcast_to(placed[32:33, here], (8, CHUNK))
        quad(spread.at[j], column_weight(j).T)

    listing.wait()
    load.wait()

    signals = (n_row - 1) + (n_col - 1)
    for down, right in diagonals:
        signals = signals + jnp.where(exists(down, right), 1, 0)
    pl.semaphore_wait(barrier, signals)

    def prepare_filters():
        for j in range(CHUNKS):
            quad(gather.at[j], column_weight(j))
        cov_high, cov_rest = split(cov_ref[...])
        eights = [
            lambda x: x >> 3,
            functools.partial(lane_step, side=0),
            functools.partial(lane_step, side=1),
        ]
        same = (iota((2 * CY, 2 * CY), 0) & 7) == (iota((2 * CY, 2 * CY), 1) & 7)
        for kind, step_of in enumerate(eights):
            tall = jnp.where(step_of(iota((2 * CY, STEPS), 0)) == iota((2 * CY, STEPS), 1), 1.0, 0.0)
            wide = jnp.where(step_of(iota((STEPS, 2 * CY), 1)) == iota((STEPS, 2 * CY), 0), 1.0, 0.0)
            tall, wide = tall.astype(bf16), wide.astype(bf16)
            for part, values in enumerate((cov_high, cov_rest)):
                block = dot(tall, dot(values, wide).astype(bf16))
                block = jnp.where(same, block, 0.0).astype(bf16)
                if kind == 0:
                    cov_time[part] = block
                else:
                    cov_side[kind - 1, part] = block
        for ref, count in ((wide_band, 96), (band_row, 64)):
            reach = count + 16
            line, place = iota((2 * count, 2 * reach), 0), iota((2 * count, 2 * reach), 1)
            above, before = line < count, place < reach
            value = taper(
                jnp.where(before, place, place - reach) - 8 - jnp.where(above, line, line - count)
            )
            high, rest = split(value)
            rest = jnp.where(before, rest.astype(f32), 0.0)
            ref[...] = jnp.where(above, high.astype(f32), rest).astype(bf16)

        line, column = iota((CY, CY), 0), iota((CY, CY), 1)
        quad(band_own, taper(line - column))
        source, target = line >> 3, column >> 3
        from_left = taper((column & 7) + 8 - (line & 7))
        from_right = taper(8 + (line & 7) - (column & 7))
        for odd in range(2):
            left = ((target & 1) == 0) & (source == target + odd)
            right = ((target & 1) == 1) & (source == ((target + 2 + odd) & 15))
            weight = jnp.where(left, from_left, 0.0) + jnp.where(right, from_right, 0.0)
            quad(band_edge.at[odd], weight)

    def row_weight(chunk, group):
        row = site_row[chunk] - 8 * group
        along = site_along[chunk]
        line = iota((8, CHUNK), 0)
        return jnp.where(row == line, 1.0 - along, 0.0) + jnp.where(row + 1 == line, along, 0.0)

    def messages(call, part):
        field, rows = merged.at[call], slice(part * PART, (part + 1) * PART)
        there = slice(8 + part * PART, 8 + (part + 1) * PART)
        table = []
        if part == 0:
            table += [
                (-1, 0, field.at[:, 0:8, :], row_halo.at[call, 1]),
                (-1, 1, pack.at[0, :, 0:8, :], col_halo.at[call, 0, :, HIGH - 8 : HIGH, :]),
                (-1, -1, pack.at[1, :, 0:8, :], col_halo.at[call, 1, :, HIGH - 8 : HIGH, :]),
            ]
        if part == PARTS - 1:
            table += [
                (1, 0, field.at[:, CX - 8 : CX, :], row_halo.at[call, 0]),
                (1, 1, pack.at[0, :, CX - 8 : CX, :], col_halo.at[call, 0, :, 0:8, :]),
                (1, -1, pack.at[1, :, CX - 8 : CX, :], col_halo.at[call, 1, :, 0:8, :]),
            ]
        table += [
            (0, 1, pack.at[0, :, rows, :], col_halo.at[call, 0, :, there, :]),
            (0, -1, pack.at[1, :, rows, :], col_halo.at[call, 1, :, there, :]),
        ]
        return [
            (
                down,
                right,
                pltpu.make_async_remote_copy(
                    src_ref=source,
                    dst_ref=target,
                    send_sem=send_sem.at[call, part, index],
                    recv_sem=recv_sem.at[call, part, index],
                    device_id=(me_row + down, me_col + right),
                    device_id_type=MESH,
                ),
            )
            for index, (down, right, source, target) in enumerate(table)
        ]

    def mix(groups):
        parts = [split(values.reshape(CX, CY)) for values in groups]
        small = dot(cov_time[1], jnp.concatenate([high for high, _ in parts], axis=1))
        return [
            (
                halves(dot(cov_time[0], jnp.concatenate(part, axis=1)))
                + small[:, index * CY : (index + 1) * CY]
            ).reshape(STEPS, 8, CY)
            for index, part in enumerate(parts)
        ]

    def own_columns(groups):
        values = jnp.concatenate([values.reshape(CX, CY) for values in groups], axis=0)
        result = halves(dot(both(values), band_own[...]))
        return [result[0:CX].reshape(STEPS, 8, CY), result[CX:].reshape(STEPS, 8, CY)]

    def others(me, count, inner):
        outer = count // inner

        def hops(step):
            far, near = step // inner, step % inner
            return min(far, outer - far) + min(near, inner - near)

        found = []
        for step in sorted(range(1, count), key=hops, reverse=True):
            far = lax.rem(me // inner + step // inner, outer)
            near = lax.rem(lax.rem(me, inner) + step % inner, inner)
            found.append((step, far * inner + near))
        return found

    def sum_start(call, parts):
        lane = iota((1, CY), 1)
        line = jnp.zeros((1, CY), f32)
        for index, part in enumerate(parts):
            part = jnp.sum(jnp.sum(part, axis=0, keepdims=True), axis=1, keepdims=True)
            line = jnp.where(lane == index, part, line)
        row_sums[call, pl.ds(me_row, 1), 0:1, :] = line[None]
        copies = []
        for step, partner in others(me_row, n_row, 4 if n_row % 4 == 0 else 1):
            copy = pltpu.make_async_remote_copy(
                src_ref=row_sums.at[call, me_row, 0:1],
                dst_ref=row_sums.at[call, me_row, 0:1],
                send_sem=row_send.at[call, step],
                recv_sem=row_recv.at[call, step],
                device_id=(partner, me_col),
                device_id_type=MESH,
            )
            copy.start()
            copies.append(copy)
        return copies

    def sum_cross(call, copies):
        for copy in copies:
            copy.wait()
        line = row_sums[call, 0, 0:1]
        for index in range(1, n_row):
            line = line + row_sums[call, index, 0:1]
        col_sums[call, pl.ds(me_col, 1), 0:1, :] = line[None]
        copies = []
        for step, partner in others(me_col, n_col, 2 if n_col % 2 == 0 else 1):
            copy = pltpu.make_async_remote_copy(
                src_ref=col_sums.at[call, me_col, 0:1],
                dst_ref=col_sums.at[call, me_col, 0:1],
                send_sem=col_send.at[call, step],
                recv_sem=col_recv.at[call, step],
                device_id=(me_row, partner),
                device_id_type=MESH,
            )
            copy.start()
            copies.append(copy)
        return copies

    def sum_end(call, copies):
        for copy in copies:
            copy.wait()
        line = col_sums[call, 0, 0:1]
        for index in range(1, n_col):
            line = line + col_sums[call, index, 0:1]
        return [line[:, index : index + 1] for index in range(3)]

    def spread_sites(sites):
        values = sites * site_live
        for j in range(CHUNKS):
            part = values[:, j * CHUNK : (j + 1) * CHUNK]
            site_value[j] = jnp.broadcast_to(part[:, None, :], (STEPS, 8, CHUNK))

        def scatter(pair, _):
            chunk, group, link = lists[0, pair], lists[1, pair], lists[2, pair]
            value = site_value[chunk] * row_weight(chunk, group)[None]
            result = dot(both(value.reshape(CX, CHUNK)), spread[chunk])
            slots[pair] = halves(result) + slots[link]
            return 0

        lax.fori_loop(0, PAIRS, scatter, 0, unroll=23)

    def exchange(call, source):
        def join(group, _):
            here = pl.ds(pl.multiple_of(8 * group, 8), 8)
            values = source[:, here, :] + slots[lists[4, group]].reshape(STEPS, 8, CY)
            merged[call, :, here, :] = values
            place = iota((8, CY), 1) >> 3
            for pair in range(2):
                ahead = jnp.zeros((8, CY), f32)
                behind = jnp.zeros((8, CY), f32)
                for step in range(16):
                    slot = 2 * (step & 7) + (step >> 3)
                    beside = (slot + 1) & 15
                    rolled = values[16 * pair + step]
                    if beside:
                        rolled = pltpu.roll(rolled, 8 * beside, 1)
                    ahead = jnp.where(place == slot, rolled, ahead)
                    behind = jnp.where(place == beside, rolled, behind)
                pack[0, pair, here, :] = ahead
                pack[1, pair, here, :] = behind
            return 0

        width = GROUPS // PARTS
        halo = []
        for part in (0, PARTS - 1, *range(1, PARTS - 1)):
            lax.fori_loop(part * width, (part + 1) * width, join, 0, unroll=8)
            ready = messages(call, part)
            for down, right, copy in ready:

                @pl.when(exists(down, right))
                def _():
                    copy.start()

            halo += ready
        return halo

    def mix_steps(call):
        def temporal(group, _):
            here = pl.ds(pl.multiple_of(16 * group, 8), 8)
            there = pl.ds(pl.multiple_of(16 * group + 8, 8), 8)
            last = pl.ds(pl.multiple_of(16 * group + 16, 8), 8)
            low, top = own_columns(mix([merged[call, :, here, :], merged[call, :, there, :]]))
            mixed[:, there, :] = low
            mixed[:, last, :] = top
            return 0

        lax.fori_loop(0, GROUPS // 2, temporal, 0, unroll=8)

    def take_halo(call, halo):
        for down, right, copy in halo:

            @pl.when(exists(down, right))
            def _():
                copy.wait_send()

            @pl.when(exists(-down, -right))
            def _():
                copy.wait_recv()

        low, top = own_columns(mix([row_halo[call, 0], row_halo[call, 1]]))
        mixed[:, 0:8, :] = low
        mixed[:, HIGH - 8 : HIGH, :] = top
        sides = []
        for side in range(2):
            values = jnp.concatenate([col_halo[call, side, 0], col_halo[call, side, 1]], axis=1)
            high, rest = split(values)
            weight = cov_side[side, 0]
            sides.append(dot(high, weight) + dot(rest, weight) + dot(high, cov_side[side, 1]))
        even = ((iota((HIGH, CY), 1) >> 3) & 1) == 0
        for pair in range(2):
            left = sides[0][:, pair * CY : (pair + 1) * CY]
            right = sides[1][:, pair * CY : (pair + 1) * CY]
            for odd, values in enumerate((jnp.where(even, left, right), jnp.where(even, right, left))):
                edges[2 * pair + odd] = halves(dot(both(values), band_edge[odd]))

    def filtered(group, slot):
        lane = iota((HIGH, CY), 1)
        inside = (lane >= REACH) & (lane < CY - REACH)
        parts = []
        for index in (slot, slot + 1):
            edge = edges[group]
            if index:
                edge = pltpu.roll(edge, CY - 16 * index, 1)
            parts.append(split(mixed[8 * group + index] + jnp.where(inside, 0.0, edge)))
        result = []
        for begin, count, band in ((0, 96, wide_band), (96, 96, wide_band), (192, 64, band_row)):
            window = slice(begin, begin + count + 16)
            stacked = [
                jnp.concatenate([high[window], rest[window]], axis=0) for high, rest in parts
            ]
            block = dot(band[...], jnp.concatenate(stacked, axis=1))
            result.append(block[0:count] + block[count : 2 * count])
        result = 0.25 * jnp.concatenate(result, axis=0)
        return [result[:, 0:CY], result[:, CY : 2 * CY]]

    def totals(body, count):
        start = (jnp.zeros((8, CY), f32),) * count

        def sweep(group, sums):
            for slot in range(0, 8, 2):
                for beside, field in enumerate(filtered(group, slot)):
                    terms = body(8 * group + slot + beside, field)
                    sums = tuple(total + fold(term) for total, term in zip(sums, terms))
            return sums

        return lax.fori_loop(0, STEPS // 8, sweep, start, unroll=2)

    def first_sweep(step, field):
        own = grid[step]
        weighted = noise_ref[...] * own
        smooth[:, step] = field.reshape(GROUPS, 8, CY)
        first[step] = field + weighted
        return own * own, merged[0, step] * field + weighted * own

    def collect_sites(sites):
        def collect(pair, _):
            chunk, group, link = lists[0, pair], lists[1, pair], lists[3, pair]
            values = both(smooth[group].reshape(CX, CY))
            result = halves(dot(values, gather[chunk])).reshape(STEPS, 8, CHUNK)
            result = result * row_weight(chunk, group)[None]
            slots[pair] = result.reshape(CX, CHUNK) + slots[link]
            return 0

        lax.fori_loop(0, PAIRS, collect, 0, unroll=23)
        for j in range(CHUNKS):
            here = slice(j * CHUNK, (j + 1) * CHUNK)
            total = jnp.sum(slots[lists[5, j]].reshape(STEPS, 8, CHUNK), axis=1)
            site_image[:, here] = site_live[:, here] * total + site_weight[:, here] * sites[:, here]

    site_live = site_extra[3:4, :]
    site_weight = site_live * site_extra[2:3, :] + (1.0 - site_live)
    start = site_first[...]

    spread_sites(start)
    halo = exchange(0, grid)
    prepare_filters()
    mix_steps(0)
    take_halo(0, halo)
    sums = totals(first_sweep, 2)
    square = start * start
    terms = square, site_weight * square
    pending = sum_start(0, [total + fold(term) for total, term in zip(sums, terms)])
    collect_sites(start)

    once = site_image[...]
    spread_sites(once)
    pending = sum_cross(0, pending)
    halo = exchange(1, first)
    restored = dot(three(once), order[...])
    site_out[...] = restored[0:STEPS] + restored[STEPS : 2 * STEPS] + restored[2 * STEPS :]
    mix_steps(1)
    norm, across, _ = sum_end(0, pending)
    alpha = norm / across
    take_halo(1, halo)

    def second_sweep(step, field):
        own, image = grid[step], first[step]
        second[step] = field + noise_ref[...] * image
        residual = own - alpha * image
        joined = merged[0, step] - alpha * merged[1, step]
        through = smooth[:, step].reshape(CX, CY) - alpha * field
        square = residual * residual
        return square, joined * through + noise_ref[...] * square, residual * image

    sums = totals(second_sweep, 3)
    residual = start - alpha * once
    square = residual * residual
    terms = square, site_weight * square, residual * once
    pending = sum_start(1, [total + fold(term) for total, term in zip(sums, terms)])
    after, applied, cross = sum_end(1, sum_cross(1, pending))
    beta = after / norm
    alpha_next = after / (applied + beta * (2.0 * cross + beta * across))
    line = iota((8, CY), 0)
    direct = alpha + alpha_next * (1.0 + beta)
    coef_out[...] = jnp.where(line == 0, direct, -(alpha * alpha_next))


def close_kernel(
    coef_ref,
    first,
    second,
    start,
    image,
    grid,
    solution_hbm,
    residual_hbm,
    sites_hbm,
    solution,
    residual,
    sites,
    sems,
):
    direct, cross = coef_ref[0:1, 0:1], coef_ref[1:2, 0:1]
    copies = []
    for part in range(STEPS // CLOSE):
        here = slice(part * CLOSE, (part + 1) * CLOSE)
        for step in range(part * CLOSE, (part + 1) * CLOSE):
            own, once = grid[step], first[step]
            solution[step] = direct * own + cross * once
            residual[step] = own - direct * once - cross * second[step]
        for kind, (source, target) in enumerate(
            ((solution, solution_hbm), (residual, residual_hbm))
        ):
            copy = pltpu.make_async_copy(source.at[here], target.at[here], sems.at[kind, part])
            copy.start()
            copies.append(copy)
    sites[...] = (direct * start[...] + cross * image[...]).reshape(STEPS, 1, SLOT)
    copy = pltpu.make_async_copy(sites, sites_hbm.at[:, 0], sems.at[2, 0])
    copy.start()
    copies.append(copy)
    for copy in copies:
        copy.wait()


def body(
    n_row,
    n_col,
    grid_obs,
    grid_noise,
    station_obs,
    station_noise,
    station_offset,
    station_cell,
    station_count,
    time_cov,
):
    vmem = pl.BlockSpec(memory_space=pltpu.VMEM)
    anywhere = pl.BlockSpec(memory_space=pl.ANY)
    field = (STEPS, CX, CY)
    dma = pltpu.SemaphoreType.DMA
    first, second, start, image, coef = pl.pallas_call(
        functools.partial(kernel, n_row, n_col),
        out_shape=(
            pltpu.VMEM(field, f32),
            pltpu.VMEM(field, f32),
            pltpu.VMEM((STEPS, SLOT), f32),
            pltpu.VMEM((STEPS, SLOT), f32),
            pltpu.VMEM((8, CY), f32),
        ),
        in_specs=[anywhere, vmem, anywhere, vmem, anywhere, vmem, vmem, vmem],
        out_specs=(vmem,) * 5,
        scratch_shapes=[
            pltpu.VMEM(field, f32),
            pltpu.VMEM((2, STEPS, CX, CY), f32),
            pltpu.VMEM((STEPS, HIGH, CY), f32),
            pltpu.VMEM((GROUPS, STEPS, 8, CY), f32),
            pltpu.VMEM((STEPS, 1, SLOT), f32),
            pltpu.VMEM((2, 1, SLOT), f32),
            pltpu.VMEM((ZERO + 1, CX, CY), f32),
            pltpu.VMEM((2, 2, CX, CY), f32),
            pltpu.VMEM((2, 2, STEPS, 8, CY), f32),
            pltpu.VMEM((2, 2, 2, HIGH, CY), f32),
            pltpu.VMEM((2, n_row, 8, CY), f32),
            pltpu.VMEM((2, n_col, 8, CY), f32),
            pltpu.VMEM((2, 2 * CY, 2 * CY), bf16),
            pltpu.VMEM((2, 2, 2 * CY, 2 * CY), bf16),
            pltpu.VMEM((192, 224), bf16),
            pltpu.VMEM((128, 160), bf16),
            pltpu.VMEM((2 * CY, 2 * CY), bf16),
            pltpu.VMEM((2, 2 * CY, 2 * CY), bf16),
            pltpu.VMEM((4, HIGH, CY), f32),
            pltpu.VMEM((CHUNKS, 2 * CY, 2 * CHUNK), bf16),
            pltpu.VMEM((CHUNKS, 2 * CY, 2 * CHUNK), bf16),
            pltpu.VMEM((SLOT, SLOT), bf16),
            pltpu.VMEM((CHUNKS, 8, CHUNK), i32),
            pltpu.VMEM((CHUNKS, 8, CHUNK), f32),
            pltpu.VMEM((CHUNKS, STEPS, 8, CHUNK), f32),
            pltpu.VMEM((STEPS, SLOT), f32),
            pltpu.VMEM((STEPS, SLOT), f32),
            pltpu.VMEM((8, SLOT), f32),
            pltpu.VMEM((8, CHUNK), i32),
            pltpu.SMEM((8, CHUNK), i32),
            dma((3,)),
            dma,
            dma((2, PARTS, 5)),
            dma((2, PARTS, 5)),
            dma((2, n_row)),
            dma((2, n_row)),
            dma((2, n_col)),
            dma((2, n_col)),
        ],
        compiler_params=pltpu.CompilerParams(
            collective_id=0, has_side_effects=True, vmem_limit_bytes=48 * 2**20
        ),
        name="kriging",
    )(
        grid_obs,
        grid_noise,
        station_obs,
        station_noise.reshape(1, SLOT),
        station_offset,
        station_cell.reshape(1, SLOT),
        station_count,
        time_cov,
    )
    solution_grid, residual_grid, solution_sites = pl.pallas_call(
        close_kernel,
        out_shape=(
            jax.ShapeDtypeStruct(field, f32),
            jax.ShapeDtypeStruct(field, f32),
            jax.ShapeDtypeStruct((STEPS, 1, 1, SLOT), f32),
        ),
        in_specs=[vmem] * 6,
        out_specs=(anywhere,) * 3,
        scratch_shapes=[
            pltpu.VMEM(field, f32),
            pltpu.VMEM(field, f32),
            pltpu.VMEM((STEPS, 1, SLOT), f32),
            dma((3, STEPS)),
        ],
        compiler_params=pltpu.CompilerParams(vmem_limit_bytes=16 * 2**20),
        name="close",
    )(coef, first, second, start, image, grid_obs)
    return solution_grid, solution_sites, residual_grid


def solution(mesh):
    placed = (
        P(None, "row", "col"),
        P("row", "col"),
        P(None, "row", "col", None),
        P("row", "col", None),
        P(None, "row", "col", None),
        P("row", "col", None),
        P("row", "col"),
        P(),
    )
    return jax.shard_map(
        functools.partial(body, mesh.shape["row"], mesh.shape["col"]),
        mesh=mesh,
        in_specs=placed,
        out_specs=(P(None, "row", "col"), P(None, "row", "col", None), P(None, "row", "col")),
        check_vma=False,
    )
```

```python
import functools

import jax
import jax.numpy as jnp
from jax import lax
from jax.experimental import pallas as pl
from jax.experimental.pallas import tpu as pltpu
from jax.sharding import PartitionSpec as P

REACH = 8
CLOSE = 2
CX = 256
CY = 128
STEPS = 32
SLOT = 1024
CHUNK = 128
CHUNKS = SLOT // CHUNK
GROUPS = CX // 8
PARTS = 4
PART = CX // PARTS
PAIRS = GROUPS + 2 * CHUNKS - 2
ZERO = PAIRS
HIGH = CX + 2 * REACH
MESH = pl.DeviceIdType.MESH
f32, bf16, i32 = jnp.float32, jnp.bfloat16, jnp.int32


def iota(shape, dim):
    return lax.broadcasted_iota(i32, shape, dim)


def taper(offset):
    distance = jnp.abs(offset)
    spread = distance.astype(f32)
    value = (1.0 - spread / (REACH + 1)) * jnp.exp(-spread / 3.0)
    return jnp.where(distance <= REACH, value, 0.0)


def split(x):
    high = x.astype(bf16)
    return high, (x - high.astype(f32)).astype(bf16)


def both(x):
    return jnp.concatenate(split(x), axis=1)


def three(x):
    high = x.astype(bf16)
    rest = x - high.astype(f32)
    middle = rest.astype(bf16)
    return jnp.concatenate([high, middle, (rest - middle.astype(f32)).astype(bf16)], axis=0)


def dot(a, b):
    return lax.dot_general(a, b, (((1,), (0,)), ((), ())), preferred_element_type=f32)


def dot_nt(a, b):
    return lax.dot_general(a, b, (((1,), (1,)), ((), ())), preferred_element_type=f32)


def quad(ref, weight):
    high, rest = split(weight)
    ref[0:CY, :] = jnp.concatenate([high, rest], axis=1)
    ref[CY : 2 * CY, :] = jnp.concatenate([high, jnp.zeros_like(high)], axis=1)


def halves(x):
    return x[:, :CY] + x[:, CY:]


def fold(x):
    rows, cols = x.shape
    total = jnp.zeros((8, CY), f32)
    for c in range(cols // CY):
        total = total + jnp.sum(x[:, c * CY : (c + 1) * CY].reshape(rows // 8, 8, CY), axis=0)
    return total


def lane_step(lane, side):
    pair = lane >> 7
    place = (lane >> 3) & 15
    slot, odd = place >> 1, place & 1
    if side == 0:
        return 16 * pair + 8 * odd + slot
    return 16 * pair + jnp.where(odd == 1, slot, 8 + ((slot + 7) & 7))


def kernel(
    n_row,
    n_col,
    grid_hbm,
    noise_hbm,
    obs_hbm,
    site_noise_hbm,
    offset_hbm,
    cell_hbm,
    count_ref,
    cov_hbm,
    first,
    second,
    start_out,
    site_out,
    coef_out,
    grid,
    noise_ref,
    site_noise_ref,
    cell_ref,
    cov_ref,
    merged,
    mixed,
    smooth,
    obs_ref,
    offset_ref,
    slots,
    pack,
    row_halo,
    col_halo,
    row_sums,
    col_sums,
    cov_time,
    cov_side,
    wide_band,
    band_row,
    band_own,
    band_edge,
    edges,
    spread,
    gather,
    order,
    site_row,
    site_along,
    site_value,
    site_first,
    site_image,
    site_extra,
    list_vmem,
    lists,
    local_sem,
    list_sem,
    send_sem,
    recv_sem,
    row_send,
    row_recv,
    col_send,
    col_recv,
):
    me_row = lax.axis_index("row")
    me_col = lax.axis_index("col")

    pairs = (
        (cell_hbm, cell_ref),
        (obs_hbm.at[:, 0], obs_ref),
        (offset_hbm.at[:, 0], offset_ref),
        (site_noise_hbm, site_noise_ref),
        (cov_hbm, cov_ref),
        (noise_hbm, noise_ref),
        (grid_hbm, grid),
    )
    loads = [
        pltpu.make_async_copy(source, target, local_sem.at[index])
        for index, (source, target) in enumerate(pairs)
    ]
    for copy in loads:
        copy.start()

    barrier = pltpu.get_barrier_semaphore()
    for step in range(1, n_row):
        pl.semaphore_signal(
            barrier, inc=1, device_id=(lax.rem(me_row + step, n_row), me_col), device_id_type=MESH
        )
    for step in range(1, n_col):
        pl.semaphore_signal(
            barrier, inc=1, device_id=(me_row, lax.rem(me_col + step, n_col)), device_id_type=MESH
        )

    def exists(down, right):
        row, col = me_row + down, me_col + right
        return (row >= 0) & (row < n_row) & (col >= 0) & (col < n_col)

    diagonals = [(-1, -1), (-1, 1), (1, -1), (1, 1)]
    for down, right in diagonals:

        @pl.when(exists(down, right))
        def _():
            pl.semaphore_signal(
                barrier, inc=1, device_id=(me_row + down, me_col + right), device_id_type=MESH
            )

    @pl.when(me_row == 0)
    def _():
        row_halo[:, 0] = jnp.zeros((2, STEPS, 8, CY), f32)
        col_halo[:, :, :, 0:8, :] = jnp.zeros((2, 2, 2, 8, CY), f32)

    @pl.when(me_row == n_row - 1)
    def _():
        row_halo[:, 1] = jnp.zeros((2, STEPS, 8, CY), f32)
        col_halo[:, :, :, HIGH - 8 : HIGH, :] = jnp.zeros((2, 2, 2, 8, CY), f32)

    @pl.when(me_col == 0)
    def _():
        col_halo[:, 0] = jnp.zeros((2, 2, HIGH, CY), f32)

    @pl.when(me_col == n_col - 1)
    def _():
        col_halo[:, 1] = jnp.zeros((2, 2, HIGH, CY), f32)

    slots[ZERO] = jnp.zeros((CX, CY), f32)

    loads[0].wait()
    cell = cell_ref[...]
    row_of = cell >> 7
    key = row_of * SLOT + iota((1, SLOT), 1)
    counts = [jnp.zeros((1, CHUNK), i32) for _ in range(CHUNKS)]
    for j in range(CHUNKS):
        own = jnp.broadcast_to(key[:, j * CHUNK : (j + 1) * CHUNK], (CHUNK, CHUNK)).T
        for k in range(CHUNKS):
            less = own < key[:, k * CHUNK : (k + 1) * CHUNK]
            counts[k] = counts[k] + jnp.sum(jnp.where(less, 1, 0), axis=0, keepdims=True)
    rank = jnp.concatenate(counts, axis=1)
    for j in range(CHUNKS):
        place = iota((CHUNK, SLOT), 0) + j * CHUNK
        order[j * CHUNK : (j + 1) * CHUNK, :] = jnp.where(place == rank, 1.0, 0.0).astype(bf16)

    lead = iota((CHUNKS, SLOT), 0) * CHUNK
    ranks = jnp.broadcast_to(rank, (CHUNKS, SLOT))
    rows_of = jnp.broadcast_to(row_of, (CHUNKS, SLOT))
    lowest = jnp.min(jnp.where(ranks >= lead, rows_of, CX), axis=1, keepdims=True) >> 3
    highest = (jnp.max(jnp.where(ranks < lead + CHUNK, rows_of, 0), axis=1, keepdims=True) + 1) >> 3
    low = [lowest[j : j + 1, :] for j in range(CHUNKS)]
    top = [highest[j : j + 1, :] for j in range(CHUNKS)]
    begin = [jnp.zeros((1, 1), i32)]
    for j in range(CHUNKS):
        begin.append(begin[j] + top[j] - low[j] + 1)
    lane = iota((1, CHUNK), 1)
    one, none = jnp.ones((1, CHUNK), i32), jnp.zeros((1, CHUNK), i32)
    chunk_of = none
    for j in range(1, CHUNKS):
        chunk_of = chunk_of + jnp.where(begin[j] <= lane, one, none)

    def choose(which, values):
        result = jnp.broadcast_to(values[0], (1, CHUNK))
        for j in range(1, CHUNKS):
            result = jnp.where(which == j, values[j], result)
        return result

    start_of = choose(chunk_of, begin)
    group_of = jnp.minimum(choose(chunk_of, low) + lane - start_of, GROUPS - 1)
    blank = jnp.full((1, 1), -1, i32)
    link = choose(chunk_of, [blank] + begin[: CHUNKS - 1]) + group_of
    link = link - choose(chunk_of, [blank] + low[:-1])
    link = jnp.where(group_of <= choose(chunk_of, [blank] + top[:-1]), link, ZERO)
    last = none - 1
    for j in range(CHUNKS):
        last = last + jnp.where(low[j] <= lane, one, none)
    final = choose(last, begin) + lane - choose(last, low)
    final = jnp.where((last >= 0) & (choose(last, top) >= lane), final, ZERO)
    ends = none
    for j in range(CHUNKS):
        ends = jnp.where(lane == j, begin[j + 1] - 1, ends)
    listed = [chunk_of, group_of, link, jnp.where(lane == start_of, ZERO, lane - 1), final, ends]
    for row, values in enumerate(listed):
        list_vmem[row : row + 1, :] = jnp.clip(values, 0, ZERO)
    list_vmem[6:8, :] = jnp.zeros((2, CHUNK), i32)
    listing = pltpu.make_async_copy(list_vmem, lists, list_sem)
    listing.start()

    for copy in loads[1:4]:
        copy.wait()
    live = jnp.where(iota((1, SLOT), 1) < count_ref[...], 1.0, 0.0)
    start_out[...] = live * obs_ref[...].reshape(STEPS, SLOT)
    carried = jnp.concatenate(
        [
            start_out[...],
            offset_ref[...].reshape(2, SLOT),
            site_noise_ref[...],
            live,
            row_of.astype(f32),
            (cell & (CY - 1)).astype(f32),
            jnp.zeros((10, SLOT), f32),
        ],
        axis=0,
    )
    placed = dot_nt(three(carried), order[...])
    placed = placed[0:48] + placed[48:96] + placed[96:144]
    site_first[...] = placed[0:STEPS]
    site_extra[...] = placed[STEPS : STEPS + 8]

    def column_weight(j):
        here = slice(j * CHUNK, (j + 1) * CHUNK)
        along, col = site_extra[1:2, here], site_extra[5:6, here].astype(i32)
        column = iota((CY, CHUNK), 0)
        weight = jnp.where(column == col, 1.0 - along, 0.0)
        return weight + jnp.where(column == col + 1, along, 0.0)

    for j in range(CHUNKS):
        here = slice(j * CHUNK, (j + 1) * CHUNK)
        site_row[j] = jnp.broadcast_to(placed[36:37, here].astype(i32), (8, CHUNK))
        site_along[j] = jnp.broadcast_to(placed[32:33, here], (8, CHUNK))
        quad(spread.at[j], column_weight(j).T)

    listing.wait()
    for copy in loads[4:]:
        copy.wait()

    signals = (n_row - 1) + (n_col - 1)
    for down, right in diagonals:
        signals = signals + jnp.where(exists(down, right), 1, 0)
    pl.semaphore_wait(barrier, signals)

    def prepare_filters():
        for j in range(CHUNKS):
            quad(gather.at[j], column_weight(j))
        cov_high, cov_rest = split(cov_ref[...])
        eights = [
            lambda x: x >> 3,
            functools.partial(lane_step, side=0),
            functools.partial(lane_step, side=1),
        ]
        same = (iota((2 * CY, 2 * CY), 0) & 7) == (iota((2 * CY, 2 * CY), 1) & 7)
        for kind, step_of in enumerate(eights):
            tall = jnp.where(step_of(iota((2 * CY, STEPS), 0)) == iota((2 * CY, STEPS), 1), 1.0, 0.0)
            wide = jnp.where(step_of(iota((STEPS, 2 * CY), 1)) == iota((STEPS, 2 * CY), 0), 1.0, 0.0)
            tall, wide = tall.astype(bf16), wide.astype(bf16)
            for part, values in enumerate((cov_high, cov_rest)):
                block = dot(tall, dot(values, wide).astype(bf16))
                block = jnp.where(same, block, 0.0).astype(bf16)
                if kind == 0:
                    cov_time[part] = block
                else:
                    cov_side[kind - 1, part] = block
        for ref, count in ((wide_band, 96), (band_row, 64)):
            reach = count + 16
            line, place = iota((2 * count, 2 * reach), 0), iota((2 * count, 2 * reach), 1)
            above, before = line < count, place < reach
            value = 0.25 * taper(
                jnp.where(before, place, place - reach) - 8 - jnp.where(above, line, line - count)
            )
            high, rest = split(value)
            rest = jnp.where(before, rest.astype(f32), 0.0)
            ref[...] = jnp.where(above, high.astype(f32), rest).astype(bf16)

        line, column = iota((CY, CY), 0), iota((CY, CY), 1)
        quad(band_own, taper(line - column))
        source, target = line >> 3, column >> 3
        from_left = taper((column & 7) + 8 - (line & 7))
        from_right = taper(8 + (line & 7) - (column & 7))
        for odd in range(2):
            left = ((target & 1) == 0) & (source == target + odd)
            right = ((target & 1) == 1) & (source == ((target + 2 + odd) & 15))
            weight = jnp.where(left, from_left, 0.0) + jnp.where(right, from_right, 0.0)
            quad(band_edge.at[odd], weight)

    def row_weight(chunk, group):
        row = site_row[chunk] - 8 * group
        along = site_along[chunk]
        line = iota((8, CHUNK), 0)
        return jnp.where(row == line, 1.0 - along, 0.0) + jnp.where(row + 1 == line, along, 0.0)

    def messages(call, part):
        field, rows = merged.at[call], slice(part * PART, (part + 1) * PART)
        there = slice(8 + part * PART, 8 + (part + 1) * PART)
        table = []
        if part == 0:
            table += [
                (-1, 0, field.at[:, 0:8, :], row_halo.at[call, 1]),
                (-1, 1, pack.at[0, :, 0:8, :], col_halo.at[call, 0, :, HIGH - 8 : HIGH, :]),
                (-1, -1, pack.at[1, :, 0:8, :], col_halo.at[call, 1, :, HIGH - 8 : HIGH, :]),
            ]
        if part == PARTS - 1:
            table += [
                (1, 0, field.at[:, CX - 8 : CX, :], row_halo.at[call, 0]),
                (1, 1, pack.at[0, :, CX - 8 : CX, :], col_halo.at[call, 0, :, 0:8, :]),
                (1, -1, pack.at[1, :, CX - 8 : CX, :], col_halo.at[call, 1, :, 0:8, :]),
            ]
        table += [
            (0, 1, pack.at[0, :, rows, :], col_halo.at[call, 0, :, there, :]),
            (0, -1, pack.at[1, :, rows, :], col_halo.at[call, 1, :, there, :]),
        ]
        return [
            (
                down,
                right,
                pltpu.make_async_remote_copy(
                    src_ref=source,
                    dst_ref=target,
                    send_sem=send_sem.at[call, part, index],
                    recv_sem=recv_sem.at[call, part, index],
                    device_id=(me_row + down, me_col + right),
                    device_id_type=MESH,
                ),
            )
            for index, (down, right, source, target) in enumerate(table)
        ]

    def mix(groups):
        parts = [split(values.reshape(CX, CY)) for values in groups]
        small = dot(cov_time[1], jnp.concatenate([high for high, _ in parts], axis=1))
        return [
            (
                halves(dot(cov_time[0], jnp.concatenate(part, axis=1)))
                + small[:, index * CY : (index + 1) * CY]
            ).reshape(STEPS, 8, CY)
            for index, part in enumerate(parts)
        ]

    def own_columns(groups):
        values = jnp.concatenate([values.reshape(CX, CY) for values in groups], axis=0)
        result = halves(dot(both(values), band_own[...]))
        return [result[0:CX].reshape(STEPS, 8, CY), result[CX:].reshape(STEPS, 8, CY)]

    def others(me, count, inner):
        outer = count // inner

        def hops(step):
            far, near = step // inner, step % inner
            return min(far, outer - far) + min(near, inner - near)

        found = []
        for step in sorted(range(1, count), key=hops, reverse=True):
            far = lax.rem(me // inner + step // inner, outer)
            near = lax.rem(lax.rem(me, inner) + step % inner, inner)
            found.append((step, far * inner + near))
        return found

    def sum_start(call, parts):
        lane = iota((1, CY), 1)
        line = jnp.zeros((1, CY), f32)
        for index, part in enumerate(parts):
            part = jnp.sum(jnp.sum(part, axis=0, keepdims=True), axis=1, keepdims=True)
            line = jnp.where(lane == index, part, line)
        row_sums[call, pl.ds(me_row, 1), 0:1, :] = line[None]
        copies = []
        for step, partner in others(me_row, n_row, 4 if n_row % 4 == 0 else 1):
            copy = pltpu.make_async_remote_copy(
                src_ref=row_sums.at[call, me_row, 0:1],
                dst_ref=row_sums.at[call, me_row, 0:1],
                send_sem=row_send.at[call, step],
                recv_sem=row_recv.at[call, step],
                device_id=(partner, me_col),
                device_id_type=MESH,
            )
            copy.start()
            copies.append(copy)
        return copies

    def sum_cross(call, copies):
        for copy in copies:
            copy.wait()
        line = row_sums[call, 0, 0:1]
        for index in range(1, n_row):
            line = line + row_sums[call, index, 0:1]
        col_sums[call, pl.ds(me_col, 1), 0:1, :] = line[None]
        copies = []
        for step, partner in others(me_col, n_col, 2 if n_col % 2 == 0 else 1):
            copy = pltpu.make_async_remote_copy(
                src_ref=col_sums.at[call, me_col, 0:1],
                dst_ref=col_sums.at[call, me_col, 0:1],
                send_sem=col_send.at[call, step],
                recv_sem=col_recv.at[call, step],
                device_id=(me_row, partner),
                device_id_type=MESH,
            )
            copy.start()
            copies.append(copy)
        return copies

    def sum_end(call, copies):
        for copy in copies:
            copy.wait()
        line = col_sums[call, 0, 0:1]
        for index in range(1, n_col):
            line = line + col_sums[call, index, 0:1]
        return [line[:, index : index + 1] for index in range(3)]

    def spread_sites(sites):
        values = sites * site_live
        for j in range(CHUNKS):
            part = values[:, j * CHUNK : (j + 1) * CHUNK]
            site_value[j] = jnp.broadcast_to(part[:, None, :], (STEPS, 8, CHUNK))

        def scatter(pair, _):
            chunk, group, link = lists[0, pair], lists[1, pair], lists[2, pair]
            value = site_value[chunk] * row_weight(chunk, group)[None]
            result = dot(both(value.reshape(CX, CHUNK)), spread[chunk])
            slots[pair] = halves(result) + slots[link]
            return 0

        lax.fori_loop(0, PAIRS, scatter, 0, unroll=23)

    def exchange(call, source):
        def join(group, _):
            here = pl.ds(pl.multiple_of(8 * group, 8), 8)
            values = source[:, here, :] + slots[lists[4, group]].reshape(STEPS, 8, CY)
            merged[call, :, here, :] = values
            place = iota((8, CY), 1) >> 3
            for pair in range(2):
                ahead = jnp.zeros((8, CY), f32)
                behind = jnp.zeros((8, CY), f32)
                for step in range(16):
                    slot = 2 * (step & 7) + (step >> 3)
                    beside = (slot + 1) & 15
                    rolled = values[16 * pair + step]
                    if beside:
                        rolled = pltpu.roll(rolled, 8 * beside, 1)
                    ahead = jnp.where(place == slot, rolled, ahead)
                    behind = jnp.where(place == beside, rolled, behind)
                pack[0, pair, here, :] = ahead
                pack[1, pair, here, :] = behind
            return 0

        width = GROUPS // PARTS
        halo = []
        for part in (0, PARTS - 1, *range(1, PARTS - 1)):
            lax.fori_loop(part * width, (part + 1) * width, join, 0, unroll=8)
            ready = messages(call, part)
            for down, right, copy in ready:

                @pl.when(exists(down, right))
                def _():
                    copy.start()

            halo += ready
        return halo

    def mix_steps(call):
        def temporal(group, _):
            here = pl.ds(pl.multiple_of(16 * group, 8), 8)
            there = pl.ds(pl.multiple_of(16 * group + 8, 8), 8)
            last = pl.ds(pl.multiple_of(16 * group + 16, 8), 8)
            low, top = own_columns(mix([merged[call, :, here, :], merged[call, :, there, :]]))
            mixed[:, there, :] = low
            mixed[:, last, :] = top
            return 0

        lax.fori_loop(0, GROUPS // 2, temporal, 0, unroll=16)

    def take_halo(call, halo):
        for down, right, copy in halo:

            @pl.when(exists(down, right))
            def _():
                copy.wait_send()

            @pl.when(exists(-down, -right))
            def _():
                copy.wait_recv()

        low, top = own_columns(mix([row_halo[call, 0], row_halo[call, 1]]))
        mixed[:, 0:8, :] = low
        mixed[:, HIGH - 8 : HIGH, :] = top
        sides = []
        for side in range(2):
            values = jnp.concatenate([col_halo[call, side, 0], col_halo[call, side, 1]], axis=1)
            high, rest = split(values)
            weight = cov_side[side, 0]
            sides.append(dot(high, weight) + dot(rest, weight) + dot(high, cov_side[side, 1]))
        even = ((iota((HIGH, CY), 1) >> 3) & 1) == 0
        for pair in range(2):
            left = sides[0][:, pair * CY : (pair + 1) * CY]
            right = sides[1][:, pair * CY : (pair + 1) * CY]
            for odd, values in enumerate((jnp.where(even, left, right), jnp.where(even, right, left))):
                edges[2 * pair + odd] = halves(dot(both(values), band_edge[odd]))

    def filtered(group, slot):
        lane = iota((HIGH, CY), 1)
        inside = (lane >= REACH) & (lane < CY - REACH)
        parts = []
        for index in (slot, slot + 1):
            edge = edges[group]
            if index:
                edge = pltpu.roll(edge, CY - 16 * index, 1)
            parts.append(split(mixed[8 * group + index] + jnp.where(inside, 0.0, edge)))
        result = []
        for begin, count, band in ((0, 96, wide_band), (96, 96, wide_band), (192, 64, band_row)):
            window = slice(begin, begin + count + 16)
            stacked = [
                jnp.concatenate([high[window], rest[window]], axis=0) for high, rest in parts
            ]
            block = dot(band[...], jnp.concatenate(stacked, axis=1))
            result.append(block[0:count] + block[count : 2 * count])
        result = jnp.concatenate(result, axis=0)
        return [result[:, 0:CY], result[:, CY : 2 * CY]]

    def totals(body, count):
        start = (jnp.zeros((8, CY), f32),) * count

        def sweep(group, sums):
            for slot in range(0, 8, 2):
                for beside, field in enumerate(filtered(group, slot)):
                    terms = body(8 * group + slot + beside, field)
                    sums = tuple(total + fold(term) for total, term in zip(sums, terms))
            return sums

        return lax.fori_loop(0, STEPS // 8, sweep, start, unroll=2)

    def first_sweep(step, field):
        own = grid[step]
        weighted = noise_ref[...] * own
        smooth[:, step] = field.reshape(GROUPS, 8, CY)
        first[step] = field + weighted
        return own * own, merged[0, step] * field + weighted * own

    def collect_sites(sites):
        def collect(pair, _):
            chunk, group, link = lists[0, pair], lists[1, pair], lists[3, pair]
            values = both(smooth[group].reshape(CX, CY))
            result = halves(dot(values, gather[chunk])).reshape(STEPS, 8, CHUNK)
            result = result * row_weight(chunk, group)[None]
            slots[pair] = result.reshape(CX, CHUNK) + slots[link]
            return 0

        lax.fori_loop(0, PAIRS, collect, 0, unroll=23)
        for j in range(CHUNKS):
            here = slice(j * CHUNK, (j + 1) * CHUNK)
            total = jnp.sum(slots[lists[5, j]].reshape(STEPS, 8, CHUNK), axis=1)
            site_image[:, here] = site_live[:, here] * total + site_weight[:, here] * sites[:, here]

    site_live = site_extra[3:4, :]
    site_weight = site_live * site_extra[2:3, :] + (1.0 - site_live)
    start = site_first[...]

    spread_sites(start)
    halo = exchange(0, grid)
    prepare_filters()
    mix_steps(0)
    take_halo(0, halo)
    sums = totals(first_sweep, 2)
    square = start * start
    terms = square, site_weight * square
    pending = sum_start(0, [total + fold(term) for total, term in zip(sums, terms)])
    collect_sites(start)

    once = site_image[...]
    spread_sites(once)
    pending = sum_cross(0, pending)
    halo = exchange(1, first)
    restored = dot(three(once), order[...])
    site_out[...] = restored[0:STEPS] + restored[STEPS : 2 * STEPS] + restored[2 * STEPS :]
    mix_steps(1)
    norm, across, _ = sum_end(0, pending)
    alpha = norm / across
    take_halo(1, halo)

    def second_sweep(step, field):
        own, image = grid[step], first[step]
        second[step] = field + noise_ref[...] * image
        residual = own - alpha * image
        joined = merged[0, step] - alpha * merged[1, step]
        through = smooth[:, step].reshape(CX, CY) - alpha * field
        square = residual * residual
        return square, joined * through + noise_ref[...] * square, residual * image

    sums = totals(second_sweep, 3)
    residual = start - alpha * once
    square = residual * residual
    terms = square, site_weight * square, residual * once
    pending = sum_start(1, [total + fold(term) for total, term in zip(sums, terms)])
    after, applied, cross = sum_end(1, sum_cross(1, pending))
    beta = after / norm
    alpha_next = after / (applied + beta * (2.0 * cross + beta * across))
    line = iota((8, CY), 0)
    direct = alpha + alpha_next * (1.0 + beta)
    coef_out[...] = jnp.where(line == 0, direct, -(alpha * alpha_next))


def close_kernel(
    coef_ref,
    first,
    second,
    start,
    image,
    grid,
    solution_hbm,
    residual_hbm,
    sites_hbm,
    solution,
    residual,
    sites,
    sems,
):
    direct, cross = coef_ref[0:1, 0:1], coef_ref[1:2, 0:1]
    copies = []
    for part in range(STEPS // CLOSE):
        here = slice(part * CLOSE, (part + 1) * CLOSE)
        for step in range(part * CLOSE, (part + 1) * CLOSE):
            own, once = grid[step], first[step]
            solution[step] = direct * own + cross * once
            residual[step] = own - direct * once - cross * second[step]
        for kind, (source, target) in enumerate(
            ((solution, solution_hbm), (residual, residual_hbm))
        ):
            copy = pltpu.make_async_copy(source.at[here], target.at[here], sems.at[kind, part])
            copy.start()
            copies.append(copy)
    sites[...] = (direct * start[...] + cross * image[...]).reshape(STEPS, 1, SLOT)
    copy = pltpu.make_async_copy(sites, sites_hbm.at[:, 0], sems.at[2, 0])
    copy.start()
    copies.append(copy)
    for copy in copies:
        copy.wait()


def body(
    n_row,
    n_col,
    grid_obs,
    grid_noise,
    station_obs,
    station_noise,
    station_offset,
    station_cell,
    station_count,
    time_cov,
):
    vmem = pl.BlockSpec(memory_space=pltpu.VMEM)
    anywhere = pl.BlockSpec(memory_space=pl.ANY)
    field = (STEPS, CX, CY)
    dma = pltpu.SemaphoreType.DMA
    first, second, start, image, coef, kept = pl.pallas_call(
        functools.partial(kernel, n_row, n_col),
        out_shape=(
            pltpu.VMEM(field, f32),
            pltpu.VMEM(field, f32),
            pltpu.VMEM((STEPS, SLOT), f32),
            pltpu.VMEM((STEPS, SLOT), f32),
            pltpu.VMEM((8, CY), f32),
            pltpu.VMEM(field, f32),
        ),
        in_specs=[anywhere] * 6 + [vmem, anywhere],
        out_specs=(vmem,) * 6,
        scratch_shapes=[
            pltpu.VMEM((CX, CY), f32),
            pltpu.VMEM((1, SLOT), f32),
            pltpu.VMEM((1, SLOT), i32),
            pltpu.VMEM((STEPS, STEPS), f32),
            pltpu.VMEM((2, STEPS, CX, CY), f32),
            pltpu.VMEM((STEPS, HIGH, CY), f32),
            pltpu.VMEM((GROUPS, STEPS, 8, CY), f32),
            pltpu.VMEM((STEPS, 1, SLOT), f32),
            pltpu.VMEM((2, 1, SLOT), f32),
            pltpu.VMEM((ZERO + 1, CX, CY), f32),
            pltpu.VMEM((2, 2, CX, CY), f32),
            pltpu.VMEM((2, 2, STEPS, 8, CY), f32),
            pltpu.VMEM((2, 2, 2, HIGH, CY), f32),
            pltpu.VMEM((2, n_row, 8, CY), f32),
            pltpu.VMEM((2, n_col, 8, CY), f32),
            pltpu.VMEM((2, 2 * CY, 2 * CY), bf16),
            pltpu.VMEM((2, 2, 2 * CY, 2 * CY), bf16),
            pltpu.VMEM((192, 224), bf16),
            pltpu.VMEM((128, 160), bf16),
            pltpu.VMEM((2 * CY, 2 * CY), bf16),
            pltpu.VMEM((2, 2 * CY, 2 * CY), bf16),
            pltpu.VMEM((4, HIGH, CY), f32),
            pltpu.VMEM((CHUNKS, 2 * CY, 2 * CHUNK), bf16),
            pltpu.VMEM((CHUNKS, 2 * CY, 2 * CHUNK), bf16),
            pltpu.VMEM((SLOT, SLOT), bf16),
            pltpu.VMEM((CHUNKS, 8, CHUNK), i32),
            pltpu.VMEM((CHUNKS, 8, CHUNK), f32),
            pltpu.VMEM((CHUNKS, STEPS, 8, CHUNK), f32),
            pltpu.VMEM((STEPS, SLOT), f32),
            pltpu.VMEM((STEPS, SLOT), f32),
            pltpu.VMEM((8, SLOT), f32),
            pltpu.VMEM((8, CHUNK), i32),
            pltpu.SMEM((8, CHUNK), i32),
            dma((7,)),
            dma,
            dma((2, PARTS, 5)),
            dma((2, PARTS, 5)),
            dma((2, n_row)),
            dma((2, n_row)),
            dma((2, n_col)),
            dma((2, n_col)),
        ],
        compiler_params=pltpu.CompilerParams(
            collective_id=0, has_side_effects=True, vmem_limit_bytes=48 * 2**20
        ),
        name="kriging",
    )(
        grid_obs,
        grid_noise,
        station_obs,
        station_noise.reshape(1, SLOT),
        station_offset,
        station_cell.reshape(1, SLOT),
        station_count,
        time_cov,
    )
    solution_grid, residual_grid, solution_sites = pl.pallas_call(
        close_kernel,
        out_shape=(
            jax.ShapeDtypeStruct(field, f32),
            jax.ShapeDtypeStruct(field, f32),
            jax.ShapeDtypeStruct((STEPS, 1, 1, SLOT), f32),
        ),
        in_specs=[vmem] * 6,
        out_specs=(anywhere,) * 3,
        scratch_shapes=[
            pltpu.VMEM(field, f32),
            pltpu.VMEM(field, f32),
            pltpu.VMEM((STEPS, 1, SLOT), f32),
            dma((3, STEPS)),
        ],
        compiler_params=pltpu.CompilerParams(vmem_limit_bytes=16 * 2**20),
        name="close",
    )(coef, first, second, start, image, kept)
    return solution_grid, solution_sites, residual_grid


def solution(mesh):
    placed = (
        P(None, "row", "col"),
        P("row", "col"),
        P(None, "row", "col", None),
        P("row", "col", None),
        P(None, "row", "col", None),
        P("row", "col", None),
        P("row", "col"),
        P(),
    )
    return jax.shard_map(
        functools.partial(body, mesh.shape["row"], mesh.shape["col"]),
        mesh=mesh,
        in_specs=placed,
        out_specs=(P(None, "row", "col"), P(None, "row", "col", None), P(None, "row", "col")),
        check_vma=False,
    )
```

```python
import functools

import jax
import jax.numpy as jnp
from jax import lax
from jax.experimental import pallas as pl
from jax.experimental.pallas import tpu as pltpu
from jax.sharding import PartitionSpec as P

REACH = 8
CLOSE = 2
CX = 256
CY = 128
STEPS = 32
SLOT = 1024
CHUNK = 128
CHUNKS = SLOT // CHUNK
GROUPS = CX // 8
PARTS = 4
PART = CX // PARTS
PAIRS = GROUPS + 2 * CHUNKS - 2
ZERO = PAIRS
HIGH = CX + 2 * REACH
MESH = pl.DeviceIdType.MESH
f32, bf16, i32 = jnp.float32, jnp.bfloat16, jnp.int32


def iota(shape, dim):
    return lax.broadcasted_iota(i32, shape, dim)


def taper(offset):
    distance = jnp.abs(offset)
    spread = distance.astype(f32)
    value = (1.0 - spread / (REACH + 1)) * jnp.exp(-spread / 3.0)
    return jnp.where(distance <= REACH, value, 0.0)


def split(x):
    high = x.astype(bf16)
    return high, (x - high.astype(f32)).astype(bf16)


def both(x):
    return jnp.concatenate(split(x), axis=1)


def three(x):
    high = x.astype(bf16)
    rest = x - high.astype(f32)
    middle = rest.astype(bf16)
    return jnp.concatenate([high, middle, (rest - middle.astype(f32)).astype(bf16)], axis=0)


def dot(a, b):
    return lax.dot_general(a, b, (((1,), (0,)), ((), ())), preferred_element_type=f32)


def dot_nt(a, b):
    return lax.dot_general(a, b, (((1,), (1,)), ((), ())), preferred_element_type=f32)


def quad(ref, weight):
    high, rest = split(weight)
    ref[0:CY, :] = jnp.concatenate([high, rest], axis=1)
    ref[CY : 2 * CY, :] = jnp.concatenate([high, jnp.zeros_like(high)], axis=1)


def halves(x):
    return x[:, :CY] + x[:, CY:]


def fold(x):
    rows, cols = x.shape
    total = jnp.zeros((8, CY), f32)
    for c in range(cols // CY):
        total = total + jnp.sum(x[:, c * CY : (c + 1) * CY].reshape(rows // 8, 8, CY), axis=0)
    return total


def lane_step(lane, side):
    pair = lane >> 7
    place = (lane >> 3) & 15
    slot, odd = place >> 1, place & 1
    if side == 0:
        return 16 * pair + 8 * odd + slot
    return 16 * pair + jnp.where(odd == 1, slot, 8 + ((slot + 7) & 7))


def kernel(
    n_row,
    n_col,
    grid_hbm,
    noise_hbm,
    obs_hbm,
    site_noise_hbm,
    offset_hbm,
    cell_hbm,
    count_ref,
    cov_hbm,
    first,
    second,
    start_out,
    site_out,
    coef_out,
    grid,
    noise_ref,
    site_noise_ref,
    cell_ref,
    cov_ref,
    merged,
    mixed,
    smooth,
    obs_ref,
    offset_ref,
    slots,
    pack,
    row_halo,
    col_halo,
    row_sums,
    col_sums,
    cov_time,
    cov_side,
    wide_band,
    band_row,
    end_band,
    middle,
    band_own,
    band_edge,
    edges,
    spread,
    gather,
    order,
    site_row,
    site_along,
    site_value,
    site_first,
    site_image,
    site_extra,
    list_vmem,
    lists,
    local_sem,
    list_sem,
    send_sem,
    recv_sem,
    row_send,
    row_recv,
    col_send,
    col_recv,
):
    me_row = lax.axis_index("row")
    me_col = lax.axis_index("col")

    pairs = (
        (cell_hbm, cell_ref),
        (obs_hbm.at[:, 0], obs_ref),
        (offset_hbm.at[:, 0], offset_ref),
        (site_noise_hbm, site_noise_ref),
        (cov_hbm, cov_ref),
        (noise_hbm, noise_ref),
        (grid_hbm, grid),
    )
    loads = [
        pltpu.make_async_copy(source, target, local_sem.at[index])
        for index, (source, target) in enumerate(pairs)
    ]
    for copy in loads:
        copy.start()

    barrier = pltpu.get_barrier_semaphore()
    for step in range(1, n_row):
        pl.semaphore_signal(
            barrier, inc=1, device_id=(lax.rem(me_row + step, n_row), me_col), device_id_type=MESH
        )
    for step in range(1, n_col):
        pl.semaphore_signal(
            barrier, inc=1, device_id=(me_row, lax.rem(me_col + step, n_col)), device_id_type=MESH
        )

    def exists(down, right):
        row, col = me_row + down, me_col + right
        return (row >= 0) & (row < n_row) & (col >= 0) & (col < n_col)

    diagonals = [(-1, -1), (-1, 1), (1, -1), (1, 1)]
    for down, right in diagonals:

        @pl.when(exists(down, right))
        def _():
            pl.semaphore_signal(
                barrier, inc=1, device_id=(me_row + down, me_col + right), device_id_type=MESH
            )

    @pl.when(me_row == 0)
    def _():
        row_halo[:, 0] = jnp.zeros((2, STEPS, 8, CY), f32)
        col_halo[:, :, :, 0:8, :] = jnp.zeros((2, 2, 2, 8, CY), f32)

    @pl.when(me_row == n_row - 1)
    def _():
        row_halo[:, 1] = jnp.zeros((2, STEPS, 8, CY), f32)
        col_halo[:, :, :, HIGH - 8 : HIGH, :] = jnp.zeros((2, 2, 2, 8, CY), f32)

    @pl.when(me_col == 0)
    def _():
        col_halo[:, 0] = jnp.zeros((2, 2, HIGH, CY), f32)

    @pl.when(me_col == n_col - 1)
    def _():
        col_halo[:, 1] = jnp.zeros((2, 2, HIGH, CY), f32)

    slots[ZERO] = jnp.zeros((CX, CY), f32)

    loads[0].wait()
    cell = cell_ref[...]
    row_of = cell >> 7
    key = row_of * SLOT + iota((1, SLOT), 1)
    counts = [jnp.zeros((1, CHUNK), i32) for _ in range(CHUNKS)]
    for j in range(CHUNKS):
        own = jnp.broadcast_to(key[:, j * CHUNK : (j + 1) * CHUNK], (CHUNK, CHUNK)).T
        for k in range(CHUNKS):
            less = own < key[:, k * CHUNK : (k + 1) * CHUNK]
            counts[k] = counts[k] + jnp.sum(jnp.where(less, 1, 0), axis=0, keepdims=True)
    rank = jnp.concatenate(counts, axis=1)
    for j in range(CHUNKS):
        place = iota((CHUNK, SLOT), 0) + j * CHUNK
        order[j * CHUNK : (j + 1) * CHUNK, :] = jnp.where(place == rank, 1.0, 0.0).astype(bf16)

    lead = iota((CHUNKS, SLOT), 0) * CHUNK
    ranks = jnp.broadcast_to(rank, (CHUNKS, SLOT))
    rows_of = jnp.broadcast_to(row_of, (CHUNKS, SLOT))
    lowest = jnp.min(jnp.where(ranks >= lead, rows_of, CX), axis=1, keepdims=True) >> 3
    highest = (jnp.max(jnp.where(ranks < lead + CHUNK, rows_of, 0), axis=1, keepdims=True) + 1) >> 3
    low = [lowest[j : j + 1, :] for j in range(CHUNKS)]
    top = [highest[j : j + 1, :] for j in range(CHUNKS)]
    begin = [jnp.zeros((1, 1), i32)]
    for j in range(CHUNKS):
        begin.append(begin[j] + top[j] - low[j] + 1)
    lane = iota((1, CHUNK), 1)
    one, none = jnp.ones((1, CHUNK), i32), jnp.zeros((1, CHUNK), i32)
    chunk_of = none
    for j in range(1, CHUNKS):
        chunk_of = chunk_of + jnp.where(begin[j] <= lane, one, none)

    def choose(which, values):
        result = jnp.broadcast_to(values[0], (1, CHUNK))
        for j in range(1, CHUNKS):
            result = jnp.where(which == j, values[j], result)
        return result

    start_of = choose(chunk_of, begin)
    group_of = jnp.minimum(choose(chunk_of, low) + lane - start_of, GROUPS - 1)
    blank = jnp.full((1, 1), -1, i32)
    link = choose(chunk_of, [blank] + begin[: CHUNKS - 1]) + group_of
    link = link - choose(chunk_of, [blank] + low[:-1])
    link = jnp.where(group_of <= choose(chunk_of, [blank] + top[:-1]), link, ZERO)
    last = none - 1
    for j in range(CHUNKS):
        last = last + jnp.where(low[j] <= lane, one, none)
    final = choose(last, begin) + lane - choose(last, low)
    final = jnp.where((last >= 0) & (choose(last, top) >= lane), final, ZERO)
    ends = none
    for j in range(CHUNKS):
        ends = jnp.where(lane == j, begin[j + 1] - 1, ends)
    listed = [chunk_of, group_of, link, jnp.where(lane == start_of, ZERO, lane - 1), final, ends]
    for row, values in enumerate(listed):
        list_vmem[row : row + 1, :] = jnp.clip(values, 0, ZERO)
    list_vmem[6:8, :] = jnp.zeros((2, CHUNK), i32)
    listing = pltpu.make_async_copy(list_vmem, lists, list_sem)
    listing.start()

    for copy in loads[1:4]:
        copy.wait()
    live = jnp.where(iota((1, SLOT), 1) < count_ref[...], 1.0, 0.0)
    start_out[...] = live * obs_ref[...].reshape(STEPS, SLOT)
    carried = jnp.concatenate(
        [
            start_out[...],
            offset_ref[...].reshape(2, SLOT),
            site_noise_ref[...],
            live,
            row_of.astype(f32),
            (cell & (CY - 1)).astype(f32),
            jnp.zeros((10, SLOT), f32),
        ],
        axis=0,
    )
    placed = dot_nt(three(carried), order[...])
    placed = placed[0:48] + placed[48:96] + placed[96:144]
    site_first[...] = placed[0:STEPS]
    site_extra[...] = placed[STEPS : STEPS + 8]

    def column_weight(j):
        here = slice(j * CHUNK, (j + 1) * CHUNK)
        along, col = site_extra[1:2, here], site_extra[5:6, here].astype(i32)
        column = iota((CY, CHUNK), 0)
        weight = jnp.where(column == col, 1.0 - along, 0.0)
        return weight + jnp.where(column == col + 1, along, 0.0)

    for j in range(CHUNKS):
        here = slice(j * CHUNK, (j + 1) * CHUNK)
        site_row[j] = jnp.broadcast_to(placed[36:37, here].astype(i32), (8, CHUNK))
        site_along[j] = jnp.broadcast_to(placed[32:33, here], (8, CHUNK))
        quad(spread.at[j], column_weight(j).T)

    listing.wait()
    for copy in loads[4:]:
        copy.wait()

    signals = (n_row - 1) + (n_col - 1)
    for down, right in diagonals:
        signals = signals + jnp.where(exists(down, right), 1, 0)
    pl.semaphore_wait(barrier, signals)

    def prepare_filters():
        for j in range(CHUNKS):
            quad(gather.at[j], column_weight(j))
        cov_high, cov_rest = split(cov_ref[...])
        eights = [
            lambda x: x >> 3,
            functools.partial(lane_step, side=0),
            functools.partial(lane_step, side=1),
        ]
        same = (iota((2 * CY, 2 * CY), 0) & 7) == (iota((2 * CY, 2 * CY), 1) & 7)
        for kind, step_of in enumerate(eights):
            tall = jnp.where(step_of(iota((2 * CY, STEPS), 0)) == iota((2 * CY, STEPS), 1), 1.0, 0.0)
            wide = jnp.where(step_of(iota((STEPS, 2 * CY), 1)) == iota((STEPS, 2 * CY), 0), 1.0, 0.0)
            tall, wide = tall.astype(bf16), wide.astype(bf16)
            for part, values in enumerate((cov_high, cov_rest)):
                block = dot(tall, dot(values, wide).astype(bf16))
                block = jnp.where(same, block, 0.0).astype(bf16)
                if kind == 0:
                    cov_time[part] = block
                else:
                    cov_side[kind - 1, part] = block
        for ref, count in ((wide_band, 96), (band_row, 32), (end_band, 16)):
            reach = count + 16
            line, place = iota((2 * count, 2 * reach), 0), iota((2 * count, 2 * reach), 1)
            above, before = line < count, place < reach
            value = 0.25 * taper(
                jnp.where(before, place, place - reach) - 8 - jnp.where(above, line, line - count)
            )
            high, rest = split(value)
            rest = jnp.where(before, rest.astype(f32), 0.0)
            ref[...] = jnp.where(above, high.astype(f32), rest).astype(bf16)

        line, column = iota((CY, CY), 0), iota((CY, CY), 1)
        quad(band_own, taper(line - column))
        source, target = line >> 3, column >> 3
        from_left = taper((column & 7) + 8 - (line & 7))
        from_right = taper(8 + (line & 7) - (column & 7))
        for odd in range(2):
            left = ((target & 1) == 0) & (source == target + odd)
            right = ((target & 1) == 1) & (source == ((target + 2 + odd) & 15))
            weight = jnp.where(left, from_left, 0.0) + jnp.where(right, from_right, 0.0)
            quad(band_edge.at[odd], weight)

    def row_weight(chunk, group):
        row = site_row[chunk] - 8 * group
        along = site_along[chunk]
        line = iota((8, CHUNK), 0)
        return jnp.where(row == line, 1.0 - along, 0.0) + jnp.where(row + 1 == line, along, 0.0)

    def messages(call, part):
        field, rows = merged.at[call], slice(part * PART, (part + 1) * PART)
        there = slice(8 + part * PART, 8 + (part + 1) * PART)
        table = []
        if part == 0:
            table += [
                (-1, 0, field.at[:, 0:8, :], row_halo.at[call, 1]),
                (-1, 1, pack.at[0, :, 0:8, :], col_halo.at[call, 0, :, HIGH - 8 : HIGH, :]),
                (-1, -1, pack.at[1, :, 0:8, :], col_halo.at[call, 1, :, HIGH - 8 : HIGH, :]),
            ]
        if part == PARTS - 1:
            table += [
                (1, 0, field.at[:, CX - 8 : CX, :], row_halo.at[call, 0]),
                (1, 1, pack.at[0, :, CX - 8 : CX, :], col_halo.at[call, 0, :, 0:8, :]),
                (1, -1, pack.at[1, :, CX - 8 : CX, :], col_halo.at[call, 1, :, 0:8, :]),
            ]
        table += [
            (0, 1, pack.at[0, :, rows, :], col_halo.at[call, 0, :, there, :]),
            (0, -1, pack.at[1, :, rows, :], col_halo.at[call, 1, :, there, :]),
        ]
        return [
            (
                down,
                right,
                pltpu.make_async_remote_copy(
                    src_ref=source,
                    dst_ref=target,
                    send_sem=send_sem.at[call, part, index],
                    recv_sem=recv_sem.at[call, part, index],
                    device_id=(me_row + down, me_col + right),
                    device_id_type=MESH,
                ),
            )
            for index, (down, right, source, target) in enumerate(table)
        ]

    def mix(groups):
        parts = [split(values.reshape(CX, CY)) for values in groups]
        small = dot(cov_time[1], jnp.concatenate([high for high, _ in parts], axis=1))
        return [
            (
                halves(dot(cov_time[0], jnp.concatenate(part, axis=1)))
                + small[:, index * CY : (index + 1) * CY]
            ).reshape(STEPS, 8, CY)
            for index, part in enumerate(parts)
        ]

    def own_columns(groups):
        values = jnp.concatenate([values.reshape(CX, CY) for values in groups], axis=0)
        result = halves(dot(both(values), band_own[...]))
        return [result[0:CX].reshape(STEPS, 8, CY), result[CX:].reshape(STEPS, 8, CY)]

    def others(me, count, inner):
        outer = count // inner

        def hops(step):
            far, near = step // inner, step % inner
            return min(far, outer - far) + min(near, inner - near)

        found = []
        for step in sorted(range(1, count), key=hops, reverse=True):
            far = lax.rem(me // inner + step // inner, outer)
            near = lax.rem(lax.rem(me, inner) + step % inner, inner)
            found.append((step, far * inner + near))
        return found

    def sum_start(call, parts):
        lane = iota((1, CY), 1)
        line = jnp.zeros((1, CY), f32)
        for index, part in enumerate(parts):
            part = jnp.sum(jnp.sum(part, axis=0, keepdims=True), axis=1, keepdims=True)
            line = jnp.where(lane == index, part, line)
        row_sums[call, pl.ds(me_row, 1), 0:1, :] = line[None]
        copies = []
        for step, partner in others(me_row, n_row, 4 if n_row % 4 == 0 else 1):
            copy = pltpu.make_async_remote_copy(
                src_ref=row_sums.at[call, me_row, 0:1],
                dst_ref=row_sums.at[call, me_row, 0:1],
                send_sem=row_send.at[call, step],
                recv_sem=row_recv.at[call, step],
                device_id=(partner, me_col),
                device_id_type=MESH,
            )
            copy.start()
            copies.append(copy)
        return copies

    def sum_cross(call, copies):
        for copy in copies:
            copy.wait()
        line = row_sums[call, 0, 0:1]
        for index in range(1, n_row):
            line = line + row_sums[call, index, 0:1]
        col_sums[call, pl.ds(me_col, 1), 0:1, :] = line[None]
        copies = []
        for step, partner in others(me_col, n_col, 2 if n_col % 2 == 0 else 1):
            copy = pltpu.make_async_remote_copy(
                src_ref=col_sums.at[call, me_col, 0:1],
                dst_ref=col_sums.at[call, me_col, 0:1],
                send_sem=col_send.at[call, step],
                recv_sem=col_recv.at[call, step],
                device_id=(me_row, partner),
                device_id_type=MESH,
            )
            copy.start()
            copies.append(copy)
        return copies

    def sum_end(call, copies):
        for copy in copies:
            copy.wait()
        line = col_sums[call, 0, 0:1]
        for index in range(1, n_col):
            line = line + col_sums[call, index, 0:1]
        return [line[:, index : index + 1] for index in range(3)]

    def spread_sites(sites):
        values = sites * site_live
        for j in range(CHUNKS):
            part = values[:, j * CHUNK : (j + 1) * CHUNK]
            site_value[j] = jnp.broadcast_to(part[:, None, :], (STEPS, 8, CHUNK))

        def scatter(pair, _):
            chunk, group, link = lists[0, pair], lists[1, pair], lists[2, pair]
            value = site_value[chunk] * row_weight(chunk, group)[None]
            result = dot(both(value.reshape(CX, CHUNK)), spread[chunk])
            slots[pair] = halves(result) + slots[link]
            return 0

        lax.fori_loop(0, PAIRS, scatter, 0, unroll=23)

    def exchange(call, source):
        def join(group, _):
            here = pl.ds(pl.multiple_of(8 * group, 8), 8)
            values = source[:, here, :] + slots[lists[4, group]].reshape(STEPS, 8, CY)
            merged[call, :, here, :] = values
            place = iota((8, CY), 1) >> 3
            for pair in range(2):
                ahead = jnp.zeros((8, CY), f32)
                behind = jnp.zeros((8, CY), f32)
                for step in range(16):
                    slot = 2 * (step & 7) + (step >> 3)
                    beside = (slot + 1) & 15
                    rolled = values[16 * pair + step]
                    if beside:
                        rolled = pltpu.roll(rolled, 8 * beside, 1)
                    ahead = jnp.where(place == slot, rolled, ahead)
                    behind = jnp.where(place == beside, rolled, behind)
                pack[0, pair, here, :] = ahead
                pack[1, pair, here, :] = behind
            return 0

        width = GROUPS // PARTS
        halo = []
        for part in (0, PARTS - 1, *range(1, PARTS - 1)):
            lax.fori_loop(part * width, (part + 1) * width, join, 0, unroll=8)
            ready = messages(call, part)
            for down, right, copy in ready:

                @pl.when(exists(down, right))
                def _():
                    copy.start()

            halo += ready
        return halo

    def mix_steps(call):
        def temporal(group, _):
            here = pl.ds(pl.multiple_of(16 * group, 8), 8)
            there = pl.ds(pl.multiple_of(16 * group + 8, 8), 8)
            last = pl.ds(pl.multiple_of(16 * group + 16, 8), 8)
            low, top = own_columns(mix([merged[call, :, here, :], merged[call, :, there, :]]))
            mixed[:, there, :] = low
            mixed[:, last, :] = top
            return 0

        lax.fori_loop(0, GROUPS // 2, temporal, 0, unroll=16)

    def sweep_rows(parts, begin, count, band):
        window = slice(begin, begin + count + 16)
        stacked = [jnp.concatenate([high[window], rest[window]], axis=0) for high, rest in parts]
        block = dot(band[...], jnp.concatenate(stacked, axis=1))
        return block[0:count] + block[count : 2 * count]

    blocks = (
        (0, 16, end_band),
        (16, 96, wide_band),
        (112, 96, wide_band),
        (208, 32, band_row),
        (240, 16, end_band),
    )

    def sweep_middle():
        def inner_rows(pair, _):
            parts = [split(mixed[2 * pair + beside, 16:CX, :]) for beside in range(2)]
            result = jnp.concatenate(
                [sweep_rows(parts, begin - 16, count, band) for begin, count, band in blocks[1:4]],
                axis=0,
            )
            middle[2 * pair] = result[:, 0:CY]
            middle[2 * pair + 1] = result[:, CY : 2 * CY]
            return 0

        lax.fori_loop(0, STEPS // 2, inner_rows, 0, unroll=16)

    def take_halo(call, halo):
        for down, right, copy in halo:

            @pl.when(exists(down, right))
            def _():
                copy.wait_send()

            @pl.when(exists(-down, -right))
            def _():
                copy.wait_recv()

        low, top = own_columns(mix([row_halo[call, 0], row_halo[call, 1]]))
        mixed[:, 0:8, :] = low
        mixed[:, HIGH - 8 : HIGH, :] = top
        sides = []
        for side in range(2):
            values = jnp.concatenate([col_halo[call, side, 0], col_halo[call, side, 1]], axis=1)
            high, rest = split(values)
            weight = cov_side[side, 0]
            sides.append(dot(high, weight) + dot(rest, weight) + dot(high, cov_side[side, 1]))
        even = ((iota((HIGH, CY), 1) >> 3) & 1) == 0
        for pair in range(2):
            left = sides[0][:, pair * CY : (pair + 1) * CY]
            right = sides[1][:, pair * CY : (pair + 1) * CY]
            packed = [
                split(halves(dot(both(values), band_edge[odd])))
                for odd, values in enumerate(
                    (jnp.where(even, left, right), jnp.where(even, right, left))
                )
            ]
            result = jnp.concatenate(
                [sweep_rows(packed, begin, count, band) for begin, count, band in blocks], axis=0
            )
            edges[2 * pair], edges[2 * pair + 1] = result[:, 0:CY], result[:, CY : 2 * CY]

    def filtered(group, slot):
        lane = iota((CX, CY), 1)
        inside = (lane >= REACH) & (lane < CY - REACH)
        ends = []
        for begin in (0, CX - 16):
            window = slice(begin, begin + 32)
            parts = [split(mixed[8 * group + slot + beside, window, :]) for beside in range(2)]
            ends.append(sweep_rows(parts, 0, 16, end_band))
        fields = []
        for beside in range(2):
            index, lanes = slot + beside, slice(beside * CY, (beside + 1) * CY)
            edge = edges[group]
            if index:
                edge = pltpu.roll(edge, CY - 16 * index, 1)
            field = jnp.concatenate(
                [ends[0][:, lanes], middle[8 * group + index], ends[1][:, lanes]], axis=0
            )
            fields.append(field + jnp.where(inside, 0.0, edge))
        return fields

    def totals(body, count):
        start = (jnp.zeros((8, CY), f32),) * count

        def sweep(group, sums):
            for slot in range(0, 8, 2):
                for beside, field in enumerate(filtered(group, slot)):
                    terms = body(8 * group + slot + beside, field)
                    sums = tuple(total + fold(term) for total, term in zip(sums, terms))
            return sums

        return lax.fori_loop(0, STEPS // 8, sweep, start, unroll=4)

    def first_sweep(step, field):
        own = grid[step]
        weighted = noise_ref[...] * own
        smooth[:, step] = field.reshape(GROUPS, 8, CY)
        first[step] = field + weighted
        return own * own, merged[0, step] * field + weighted * own

    def collect_sites(sites):
        def collect(pair, _):
            chunk, group, link = lists[0, pair], lists[1, pair], lists[3, pair]
            values = both(smooth[group].reshape(CX, CY))
            result = halves(dot(values, gather[chunk])).reshape(STEPS, 8, CHUNK)
            result = result * row_weight(chunk, group)[None]
            slots[pair] = result.reshape(CX, CHUNK) + slots[link]
            return 0

        lax.fori_loop(0, PAIRS, collect, 0, unroll=23)
        for j in range(CHUNKS):
            here = slice(j * CHUNK, (j + 1) * CHUNK)
            total = jnp.sum(slots[lists[5, j]].reshape(STEPS, 8, CHUNK), axis=1)
            site_image[:, here] = site_live[:, here] * total + site_weight[:, here] * sites[:, here]

    site_live = site_extra[3:4, :]
    site_weight = site_live * site_extra[2:3, :] + (1.0 - site_live)
    start = site_first[...]

    spread_sites(start)
    halo = exchange(0, grid)
    prepare_filters()
    mix_steps(0)
    sweep_middle()
    take_halo(0, halo)
    sums = totals(first_sweep, 2)
    square = start * start
    terms = square, site_weight * square
    pending = sum_start(0, [total + fold(term) for total, term in zip(sums, terms)])
    collect_sites(start)

    once = site_image[...]
    spread_sites(once)
    pending = sum_cross(0, pending)
    halo = exchange(1, first)
    restored = dot(three(once), order[...])
    site_out[...] = restored[0:STEPS] + restored[STEPS : 2 * STEPS] + restored[2 * STEPS :]
    mix_steps(1)
    sweep_middle()
    norm, across, _ = sum_end(0, pending)
    alpha = norm / across
    take_halo(1, halo)

    def second_sweep(step, field):
        own, image = grid[step], first[step]
        second[step] = field + noise_ref[...] * image
        residual = own - alpha * image
        joined = merged[0, step] - alpha * merged[1, step]
        through = smooth[:, step].reshape(CX, CY) - alpha * field
        square = residual * residual
        return square, joined * through + noise_ref[...] * square, residual * image

    sums = totals(second_sweep, 3)
    residual = start - alpha * once
    square = residual * residual
    terms = square, site_weight * square, residual * once
    pending = sum_start(1, [total + fold(term) for total, term in zip(sums, terms)])
    after, applied, cross = sum_end(1, sum_cross(1, pending))
    beta = after / norm
    alpha_next = after / (applied + beta * (2.0 * cross + beta * across))
    line = iota((8, CY), 0)
    direct = alpha + alpha_next * (1.0 + beta)
    coef_out[...] = jnp.where(line == 0, direct, -(alpha * alpha_next))


def close_kernel(
    coef_ref,
    first,
    second,
    start,
    image,
    grid,
    solution_hbm,
    residual_hbm,
    sites_hbm,
    solution,
    residual,
    sites,
    sems,
):
    direct, cross = coef_ref[0:1, 0:1], coef_ref[1:2, 0:1]
    copies = []
    for part in range(STEPS // CLOSE):
        here = slice(part * CLOSE, (part + 1) * CLOSE)
        for step in range(part * CLOSE, (part + 1) * CLOSE):
            own, once = grid[step], first[step]
            solution[step] = direct * own + cross * once
            residual[step] = own - direct * once - cross * second[step]
        for kind, (source, target) in enumerate(
            ((solution, solution_hbm), (residual, residual_hbm))
        ):
            copy = pltpu.make_async_copy(source.at[here], target.at[here], sems.at[kind, part])
            copy.start()
            copies.append(copy)
    sites[...] = (direct * start[...] + cross * image[...]).reshape(STEPS, 1, SLOT)
    copy = pltpu.make_async_copy(sites, sites_hbm.at[:, 0], sems.at[2, 0])
    copy.start()
    copies.append(copy)
    for copy in copies:
        copy.wait()


def body(
    n_row,
    n_col,
    grid_obs,
    grid_noise,
    station_obs,
    station_noise,
    station_offset,
    station_cell,
    station_count,
    time_cov,
):
    vmem = pl.BlockSpec(memory_space=pltpu.VMEM)
    anywhere = pl.BlockSpec(memory_space=pl.ANY)
    field = (STEPS, CX, CY)
    dma = pltpu.SemaphoreType.DMA
    first, second, start, image, coef, kept = pl.pallas_call(
        functools.partial(kernel, n_row, n_col),
        out_shape=(
            pltpu.VMEM(field, f32),
            pltpu.VMEM(field, f32),
            pltpu.VMEM((STEPS, SLOT), f32),
            pltpu.VMEM((STEPS, SLOT), f32),
            pltpu.VMEM((8, CY), f32),
            pltpu.VMEM(field, f32),
        ),
        in_specs=[anywhere] * 6 + [vmem, anywhere],
        out_specs=(vmem,) * 6,
        scratch_shapes=[
            pltpu.VMEM((CX, CY), f32),
            pltpu.VMEM((1, SLOT), f32),
            pltpu.VMEM((1, SLOT), i32),
            pltpu.VMEM((STEPS, STEPS), f32),
            pltpu.VMEM((2, STEPS, CX, CY), f32),
            pltpu.VMEM((STEPS, HIGH, CY), f32),
            pltpu.VMEM((GROUPS, STEPS, 8, CY), f32),
            pltpu.VMEM((STEPS, 1, SLOT), f32),
            pltpu.VMEM((2, 1, SLOT), f32),
            pltpu.VMEM((ZERO + 1, CX, CY), f32),
            pltpu.VMEM((2, 2, CX, CY), f32),
            pltpu.VMEM((2, 2, STEPS, 8, CY), f32),
            pltpu.VMEM((2, 2, 2, HIGH, CY), f32),
            pltpu.VMEM((2, n_row, 8, CY), f32),
            pltpu.VMEM((2, n_col, 8, CY), f32),
            pltpu.VMEM((2, 2 * CY, 2 * CY), bf16),
            pltpu.VMEM((2, 2, 2 * CY, 2 * CY), bf16),
            pltpu.VMEM((192, 224), bf16),
            pltpu.VMEM((64, 96), bf16),
            pltpu.VMEM((32, 64), bf16),
            pltpu.VMEM((STEPS, CX - 32, CY), f32),
            pltpu.VMEM((2 * CY, 2 * CY), bf16),
            pltpu.VMEM((2, 2 * CY, 2 * CY), bf16),
            pltpu.VMEM((4, CX, CY), f32),
            pltpu.VMEM((CHUNKS, 2 * CY, 2 * CHUNK), bf16),
            pltpu.VMEM((CHUNKS, 2 * CY, 2 * CHUNK), bf16),
            pltpu.VMEM((SLOT, SLOT), bf16),
            pltpu.VMEM((CHUNKS, 8, CHUNK), i32),
            pltpu.VMEM((CHUNKS, 8, CHUNK), f32),
            pltpu.VMEM((CHUNKS, STEPS, 8, CHUNK), f32),
            pltpu.VMEM((STEPS, SLOT), f32),
            pltpu.VMEM((STEPS, SLOT), f32),
            pltpu.VMEM((8, SLOT), f32),
            pltpu.VMEM((8, CHUNK), i32),
            pltpu.SMEM((8, CHUNK), i32),
            dma((7,)),
            dma,
            dma((2, PARTS, 5)),
            dma((2, PARTS, 5)),
            dma((2, n_row)),
            dma((2, n_row)),
            dma((2, n_col)),
            dma((2, n_col)),
        ],
        compiler_params=pltpu.CompilerParams(
            collective_id=0, has_side_effects=True, vmem_limit_bytes=48 * 2**20
        ),
        name="kriging",
    )(
        grid_obs,
        grid_noise,
        station_obs,
        station_noise.reshape(1, SLOT),
        station_offset,
        station_cell.reshape(1, SLOT),
        station_count,
        time_cov,
    )
    solution_grid, residual_grid, solution_sites = pl.pallas_call(
        close_kernel,
        out_shape=(
            jax.ShapeDtypeStruct(field, f32),
            jax.ShapeDtypeStruct(field, f32),
            jax.ShapeDtypeStruct((STEPS, 1, 1, SLOT), f32),
        ),
        in_specs=[vmem] * 6,
        out_specs=(anywhere,) * 3,
        scratch_shapes=[
            pltpu.VMEM(field, f32),
            pltpu.VMEM(field, f32),
            pltpu.VMEM((STEPS, 1, SLOT), f32),
            dma((3, STEPS)),
        ],
        compiler_params=pltpu.CompilerParams(vmem_limit_bytes=16 * 2**20),
        name="close",
    )(coef, first, second, start, image, kept)
    return solution_grid, solution_sites, residual_grid


def solution(mesh):
    placed = (
        P(None, "row", "col"),
        P("row", "col"),
        P(None, "row", "col", None),
        P("row", "col", None),
        P(None, "row", "col", None),
        P("row", "col", None),
        P("row", "col"),
        P(),
    )
    return jax.shard_map(
        functools.partial(body, mesh.shape["row"], mesh.shape["col"]),
        mesh=mesh,
        in_specs=placed,
        out_specs=(P(None, "row", "col"), P(None, "row", "col", None), P(None, "row", "col")),
        check_vma=False,
    )
```
